128 devices in a mesh: rows: 32 (over x, z, core), cols: 4 (over y).
Axes of the slice: x: 4, y: 4, z: 4, core: 2. Of those that a mesh axis runs over, the one named last changes fastest.
Arguments:
- panel: float32 [524288, 256], P(('rows', 'cols')), as said below
- trailing: float32 [524288, 512], P('rows', 'cols'), may hold values from -6 to 6
Outputs:
- r_factor: float32 [256, 256], replicated
- r_cross: float32 [256, 512], P(None, 'cols')
- residual: float32 [524288, 512], P('rows', 'cols')
The draws below stay inside these ranges and needn't reach their ends.
Inputs may be any that keep to these rules, and one draw needn't show every extreme that they name: The panel has full rank and is well conditioned.
All inputs are finite; a program needn't handle non-finite values.
Results may differ from the reference program's by a relative error of at most 0.0003.
Values sent between devices are 32-bit elements; how exact they have to be, the bound alone decides.
A program may use at most 256 MiB of HBM per device.

```python
import jax
import jax.numpy as jnp
from jax import lax

PANEL = 256
TRAIL = 512
ROWS = 524288


def draw_panel(key, part):
    key = jax.random.fold_in(key, 7)
    key_base, key_mix = jax.random.split(key, 2)
    position = jnp.arange(ROWS, dtype=jnp.float32) / ROWS
    base = jax.random.normal(key_base, (ROWS, PANEL + 8), jnp.float32)
    row_scale = 0.6 + 1.2 * position
    weights = jax.random.uniform(key_mix, (2, PANEL), jnp.float32, 0.15, 0.3)
    columns = base[:, :PANEL] + weights[0][None, :] * base[:, 1:PANEL + 1] + weights[1][None, :] * base[:, 5:PANEL + 5]
    return columns * row_scale[:, None] * ROWS ** (-0.5)


def level_of(rng, extent, cuts, smallest, largest):
    factor_of, own = 1.0, jax.random.fold_in(rng, 6)
    for axis_at, shards_of in cuts:
        steps = jnp.exp(jax.random.uniform(jax.random.fold_in(own, axis_at), (shards_of,), jnp.float32, smallest / len(cuts), largest / len(cuts)))
        factor_of = factor_of * jnp.repeat(steps, extent[axis_at] // shards_of).reshape([-1 if axis == axis_at else 1 for axis in range(len(extent))])
    return factor_of


def bell_draw(own_key, shape, scale, most, shards=(), kind=jnp.bfloat16):
    result = jax.random.normal(own_key, shape, jnp.float32) * scale
    if len(shards) > 0:
        result = level_of(own_key, shape, shards, -0.22, 0.18) * result
    return jnp.clip(result, min=-most, max=most).astype(kind)


def setup_inputs(seed: int = 0) -> dict:
    splits = jax.random.split(jax.random.key(seed), 3)
    panel = draw_panel(jax.random.fold_in(splits[2], 71), 0)
    trailing = bell_draw(splits[1], (ROWS, TRAIL), 1.0, 6.0, ((0, 32), (1, 4)), jnp.float32)
    return dict(panel=panel, trailing=trailing)


def reference(panel, trailing):
    q_factor, r_factor = jnp.linalg.qr(panel)
    signs = jnp.sign(jnp.diagonal(r_factor))
    r_factor = signs[:, None] * r_factor
    q_factor = q_factor * signs[None, :]
    r_cross = jnp.dot(q_factor.T.astype(jnp.float32), trailing.astype(jnp.float32), precision=lax.Precision.HIGHEST, preferred_element_type=jnp.float32)
    residual = trailing - jnp.dot(q_factor.astype(jnp.float32), r_cross.astype(jnp.float32), precision=lax.Precision.HIGHEST, preferred_element_type=jnp.float32)
    return (r_factor, r_cross, residual)
```

```python
import functools

import jax
import jax.numpy as jnp
from jax import lax
from jax.experimental import pallas as pl
from jax.experimental.pallas import tpu as pltpu
from jax.sharding import PartitionSpec as P

MESH = pl.DeviceIdType.MESH
BLOCK = 32


def split(x):
    high = x.astype(jnp.bfloat16)
    return high, (x - high.astype(jnp.float32)).astype(jnp.bfloat16)


def dot(a, b):
    return jnp.dot(a, b, preferred_element_type=jnp.float32)


def exact(a, b, dims):
    return lax.dot_general(
        a, b, (dims, ((), ())), precision=lax.Precision.HIGHEST, preferred_element_type=jnp.float32
    )


def loop(n, body):
    def step(i, carry):
        body(i)
        return carry

    lax.fori_loop(0, n, step, 0)


def factor(work, width):
    def block_step(k, carry):
        first = pl.multiple_of(k * BLOCK, BLOCK)
        rows = work[pl.ds(first, BLOCK), :]
        row_at = lax.broadcasted_iota(jnp.int32, (BLOCK, 1), 0)
        lane_at = lax.broadcasted_iota(jnp.int32, (BLOCK, width), 1)
        for j in range(BLOCK):
            column = jnp.sum(
                jnp.where(lane_at == first + j, rows[:, :width], 0.0), axis=1, keepdims=True
            )
            pivot = column[j : j + 1, :]
            scale = lax.rsqrt(pivot)
            scale = scale * (1.5 - 0.5 * pivot * scale * scale)
            pivot_row = rows[j : j + 1, :] * scale
            below = jnp.where(row_at > j, column * scale, 0.0)
            rows = jnp.where(row_at == j, pivot_row, rows - below * pivot_row)
        work[pl.ds(first, BLOCK), :] = rows
        later = jnp.where(lane_at >= first + BLOCK, rows[:, :width], 0.0)
        work[...] -= exact(later, rows, ((0,), (0,)))
        return carry

    lax.fori_loop(0, width // BLOCK, block_step, 0)


def kernel(
    groups, chunk,
    panel, trailing, r_factor, r_cross, residual,
    held, trail, high, low, turned, gram, gram_in, gram_y, gram_all, work, both,
    acc, cross_out, cross_in, cross_all,
    own_sem, trail_sem, out_sem,
    send_r, send_l, recv_l, recv_r, pass_send_r, pass_send_l, pass_recv_l, pass_recv_r,
    small_send, small_recv,
):
    width = panel.shape[1]
    columns = trailing.shape[1]
    own = panel.shape[0] // chunk
    half = own // 2
    chunks = trailing.shape[0] // chunk
    part = width // groups
    me = lax.axis_index("rows")
    y = lax.axis_index("cols")
    sides = trailing.shape[0] // panel.shape[0]
    right = lax.rem(y + 1, sides)
    left = lax.rem(y + sides - 1, sides)
    across = lax.rem(y + 2, sides)

    def load_panel(c):
        return pltpu.make_async_copy(
            panel.at[pl.ds(c * chunk, chunk)], held.at[y * own + c], own_sem.at[c]
        )

    def load_trail(c):
        return pltpu.make_async_copy(
            trailing.at[pl.ds(c * chunk, chunk)], trail.at[c], trail_sem.at[c]
        )

    def store(c):
        return pltpu.make_async_copy(
            trail.at[c], residual.at[pl.ds(c * chunk, chunk)], out_sem.at[c]
        )

    loop(own, lambda c: load_panel(c).start())
    loop(chunks, lambda c: load_trail(c).start())

    def peer(d):
        return lax.rem(me + d + 1, groups)

    def side(d):
        return lax.rem(y + d + 1, sides)

    barrier = pltpu.get_barrier_semaphore()
    loop(sides - 1, lambda d: pl.semaphore_signal(
        barrier, inc=1, device_id={"cols": side(d)}, device_id_type=MESH))
    loop(groups - 1, lambda d: pl.semaphore_signal(
        barrier, inc=1, device_id={"rows": peer(d)}, device_id_type=MESH))
    pl.semaphore_wait(barrier, groups + sides - 2)

    def copy_y(src, dst, send, recv, to):
        return pltpu.make_async_remote_copy(
            src_ref=src, dst_ref=dst, send_sem=send, recv_sem=recv,
            device_id={"cols": to}, device_id_type=MESH)

    def to_right(c):
        return copy_y(panel.at[pl.ds(c * chunk, chunk)], held.at[y * own + c],
                      send_r.at[c], recv_l.at[c], right)

    def to_left(c):
        return copy_y(panel.at[pl.ds(c * chunk, chunk)], held.at[y * own + c],
                      send_l.at[c], recv_r.at[c], left)

    def from_left(c):
        return copy_y(held.at[left * own + c], held.at[left * own + c],
                      send_r.at[c], recv_l.at[c], right)

    def from_right(c):
        return copy_y(held.at[right * own + c], held.at[right * own + c],
                      send_l.at[c], recv_r.at[c], left)

    def pass_right(c):
        return copy_y(held.at[left * own + c], held.at[left * own + c],
                      pass_send_r.at[c], pass_recv_l.at[c], right)

    def pass_left(c):
        return copy_y(held.at[right * own + half + c], held.at[right * own + half + c],
                      pass_send_l.at[c], pass_recv_r.at[c], left)

    def passed_left(c):
        return copy_y(held.at[across * own + c], held.at[across * own + c],
                      pass_send_r.at[c], pass_recv_l.at[c], right)

    def passed_right(c):
        return copy_y(held.at[across * own + half + c], held.at[across * own + half + c],
                      pass_send_l.at[c], pass_recv_r.at[c], left)

    def send_own(c):
        to_right(c).start()
        to_left(lax.rem(c + half, own)).start()

    loop(own, send_own)

    gram[...] = jnp.zeros_like(gram)
    both[...] = jnp.zeros_like(both)

    def gram_step(c):
        load_panel(c).wait()
        at = y * own + c
        x = held[at]
        x_high, x_low = split(x)
        high[at] = x_high
        low[at] = x_low
        x_turned = x.T.astype(jnp.bfloat16)
        gram[...] += dot(x_turned, x_high)
        both[:width, :] += dot(x_turned, x_low)

    loop(own, gram_step)
    mixed = both[:width, :]
    gram[...] += mixed + mixed.T

    def spread(src_of, dst, stage):
        def one(d):
            to = peer(d)
            pltpu.make_async_remote_copy(
                src_ref=src_of(to), dst_ref=dst.at[me],
                send_sem=small_send.at[stage], recv_sem=small_recv.at[stage],
                device_id={"rows": to}, device_id_type=MESH).start()

        loop(groups - 1, one)

    def spread_wait(dst, stage):
        some = dst.at[pl.ds(0, groups - 1)]
        everything = pltpu.make_async_remote_copy(
            src_ref=some, dst_ref=some,
            send_sem=small_send.at[stage], recv_sem=small_recv.at[stage],
            device_id={"rows": peer(0)}, device_id_type=MESH)
        everything.wait()

    spread(lambda to: gram.at[pl.ds(pl.multiple_of(to * part, 8), part)], gram_in, 0)
    gram_in[me] = gram[pl.ds(pl.multiple_of(me * part, 8), part), :]

    def turn(c):
        load_trail(c).wait()
        t_high, t_low = split(trail[c].T)
        turned[c, :columns, :] = t_high
        turned[c, columns:, :] = t_low

    loop(chunks, turn)
    spread_wait(gram_in, 0)
    gram_y[y] = jnp.sum(gram_in[...], axis=0)

    def over_y(d):
        return copy_y(gram_y.at[y], gram_y.at[y], small_send.at[1], small_recv.at[1], side(d))

    loop(sides - 1, lambda d: over_y(d).start())

    acc[...] = jnp.zeros_like(acc)

    def add_cross(at):
        product = dot(turned[at], high[at])
        acc[...] += product[:columns] + (
            product[columns:] + dot(turned[at, :columns, :], low[at]))

    loop(own, lambda c: add_cross(y * own + c))

    some = gram_y.at[pl.ds(0, sides - 1)]
    copy_y(some, some, small_send.at[1], small_recv.at[1], right).wait()
    gram_all[me] = jnp.sum(gram_y[...], axis=0)
    spread(lambda to: gram_all.at[me], gram_all, 2)
    spread_wait(gram_all, 2)

    row_at = lax.broadcasted_iota(jnp.int32, (width, width), 0)
    col_at = lax.broadcasted_iota(jnp.int32, (width, width), 1)
    work[:, :width] = gram_all[...].reshape(width, width)
    work[:, width:] = jnp.where(row_at == col_at, 1.0, 0.0)
    factor(work, width)
    r_factor[...] = jnp.where(row_at <= col_at, work[:, :width], 0.0)
    inverse = work[:, width:]
    both[:width, :] = inverse
    both[width:, :] = exact(inverse, inverse, ((0,), (0,)))

    def take(at):
        x_high, x_low = split(held[at])
        high[at] = x_high
        low[at] = x_low
        add_cross(at)

    def first_half(c):
        from_left(c).wait_recv()
        pass_right(c).start()
        from_right(half + c).wait_recv()
        pass_left(c).start()
        take(left * own + c)
        take(right * own + half + c)

    def second_half(c):
        from_left(half + c).wait_recv()
        take(left * own + half + c)
        from_right(c).wait_recv()
        take(right * own + c)

    def passed(c):
        passed_left(c).wait_recv()
        take(across * own + c)
        passed_right(c).wait_recv()
        take(across * own + half + c)

    loop(half, first_half)
    loop(half, second_half)
    loop(half, passed)

    for side_at in range(width // 128):
        cross_out[pl.ds(side_at * columns, columns), :] = acc[:, side_at * 128 : side_at * 128 + 128]
    spread(lambda to: cross_out.at[pl.ds(pl.multiple_of(to * part, 8), part)], cross_in, 3)
    cross_in[me] = cross_out[pl.ds(pl.multiple_of(me * part, 8), part), :]
    spread_wait(cross_in, 3)
    cross_all[me] = jnp.sum(cross_in[...], axis=0)
    spread(lambda to: cross_all.at[me], cross_all, 4)
    spread_wait(cross_all, 4)

    flat = cross_all[...].reshape(width, columns)
    cross = jnp.concatenate([flat[:columns], flat[columns:]], axis=1)
    solved = exact(both[...], cross, ((1,), (1,)))
    r_cross[...] = solved[:width]
    c_high, c_low = split(solved[width:])
    c_both = jnp.concatenate([c_high, c_low], axis=1)

    def project(c):
        product = dot(high[c], c_both)
        rest = product[:, columns:] + dot(low[c], c_high)
        trail[c] = trail[c] - (product[:, :columns] + rest)
        store(c).start()

    loop(chunks, project)

    def finish(c):
        to_right(c).wait_send()
        to_left(c).wait_send()

    loop(own, finish)

    def finish_passed(c):
        pass_right(c).wait_send()
        pass_left(c).wait_send()

    loop(half, finish_passed)
    loop(chunks, lambda c: store(c).wait())


def per_device(groups, chunk, panel, trailing):
    rows, width = panel.shape
    total, columns = trailing.shape
    own, chunks, part = rows // chunk, total // chunk, width // groups
    half = own // 2
    sides = total // rows
    f32, bf16 = jnp.float32, jnp.bfloat16
    dma = pltpu.SemaphoreType.DMA
    return pl.pallas_call(
        functools.partial(kernel, groups, chunk),
        out_shape=(
            jax.ShapeDtypeStruct((width, width), f32),
            jax.ShapeDtypeStruct((width, columns), f32),
            jax.ShapeDtypeStruct((total, columns), f32),
        ),
        in_specs=[pl.BlockSpec(memory_space=pl.ANY)] * 2,
        out_specs=(
            pl.BlockSpec(memory_space=pltpu.VMEM),
            pl.BlockSpec(memory_space=pltpu.VMEM),
            pl.BlockSpec(memory_space=pl.ANY),
        ),
        scratch_shapes=[
            pltpu.VMEM((chunks, chunk, width), f32),
            pltpu.VMEM((chunks, chunk, columns), f32),
            pltpu.VMEM((chunks, chunk, width), bf16),
            pltpu.VMEM((chunks, chunk, width), bf16),
            pltpu.VMEM((chunks, 2 * columns, chunk), bf16),
            pltpu.VMEM((width, width), f32),
            pltpu.VMEM((groups, part, width), f32),
            pltpu.VMEM((sides, part, width), f32),
            pltpu.VMEM((groups, part, width), f32),
            pltpu.VMEM((width, 2 * width), f32),
            pltpu.VMEM((2 * width, width), f32),
            pltpu.VMEM((columns, width), f32),
            pltpu.VMEM((width, columns), f32),
            pltpu.VMEM((groups, part, columns), f32),
            pltpu.VMEM((groups, part, columns), f32),
            dma((own,)), dma((chunks,)), dma((chunks,)),
            dma((own,)), dma((own,)), dma((own,)), dma((own,)),
            dma((half,)), dma((half,)), dma((half,)), dma((half,)),
            dma((5,)), dma((5,)),
        ],
        compiler_params=pltpu.CompilerParams(
            collective_id=0, has_side_effects=True, vmem_limit_bytes=60 * 2**20
        ),
    )(panel, trailing)


def solution(mesh):
    return jax.shard_map(
        functools.partial(per_device, mesh.shape["rows"], 512),
        mesh=mesh,
        in_specs=(P(("rows", "cols"), None), P("rows", "cols")),
        out_specs=(P(), P(None, "cols"), P("rows", "cols")),
        check_vma=False,
    )
```

```python
import functools

import jax
import jax.numpy as jnp
from jax import lax
from jax.experimental import pallas as pl
from jax.experimental.pallas import tpu as pltpu
from jax.sharding import PartitionSpec as P

MESH = pl.DeviceIdType.MESH
BLOCK = 32


def split(x):
    high = x.astype(jnp.bfloat16)
    return high, (x - high.astype(jnp.float32)).astype(jnp.bfloat16)


def dot(a, b):
    return jnp.dot(a, b, preferred_element_type=jnp.float32)


def exact(a, b, dims):
    return lax.dot_general(
        a, b, (dims, ((), ())), precision=lax.Precision.HIGHEST, preferred_element_type=jnp.float32
    )


def loop(n, body):
    def step(i, carry):
        body(i)
        return carry

    lax.fori_loop(0, n, step, 0)


def factor(work, width):
    def block_step(k, carry):
        first = pl.multiple_of(k * BLOCK, BLOCK)
        rows = work[pl.ds(first, BLOCK), :]
        row_at = lax.broadcasted_iota(jnp.int32, (BLOCK, 1), 0)
        lane_at = lax.broadcasted_iota(jnp.int32, (BLOCK, width), 1)
        for j in range(BLOCK):
            column = jnp.sum(
                jnp.where(lane_at == first + j, rows[:, :width], 0.0), axis=1, keepdims=True
            )
            pivot = column[j : j + 1, :]
            scale = lax.rsqrt(pivot)
            scale = scale * (1.5 - 0.5 * pivot * scale * scale)
            pivot_row = rows[j : j + 1, :] * scale
            below = jnp.where(row_at > j, column * scale, 0.0)
            rows = jnp.where(row_at == j, pivot_row, rows - below * pivot_row)
        work[pl.ds(first, BLOCK), :] = rows
        later = jnp.where(lane_at >= first + BLOCK, rows[:, :width], 0.0)
        work[...] -= exact(later, rows, ((0,), (0,)))
        return carry

    lax.fori_loop(0, width // BLOCK, block_step, 0)


def kernel(
    groups, chunk,
    panel, trailing, r_factor, r_cross, coeff, trail, high, low,
    held, turned, gram, gram_in, gram_y, gram_all, work, both,
    acc, cross_out, cross_in, cross_all,
    own_sem, trail_sem,
    send_r, send_l, recv_l, recv_r, pass_send_r, pass_send_l, pass_recv_l, pass_recv_r,
    small_send, small_recv,
):
    width = panel.shape[1]
    columns = trailing.shape[1]
    own = panel.shape[0] // chunk
    half = own // 2
    early = max(own * 3 // 8, 1)
    chunks = trailing.shape[0] // chunk
    part = width // groups
    me = lax.axis_index("rows")
    y = lax.axis_index("cols")
    sides = trailing.shape[0] // panel.shape[0]
    right = lax.rem(y + 1, sides)
    left = lax.rem(y + sides - 1, sides)
    across = lax.rem(y + 2, sides)

    def load_panel(c):
        return pltpu.make_async_copy(
            panel.at[pl.ds(c * chunk, chunk)], held.at[y * own + c], own_sem.at[c]
        )

    def load_trail(c):
        return pltpu.make_async_copy(
            trailing.at[pl.ds(c * chunk, chunk)], trail.at[c], trail_sem.at[c]
        )

    loop(own, lambda c: load_panel(c).start())
    loop(chunks, lambda c: load_trail(c).start())

    def peer(d):
        return lax.rem(me + d + 1, groups)

    def side(d):
        return lax.rem(y + d + 1, sides)

    barrier = pltpu.get_barrier_semaphore()
    loop(sides - 1, lambda d: pl.semaphore_signal(
        barrier, inc=1, device_id={"cols": side(d)}, device_id_type=MESH))
    loop(groups - 1, lambda d: pl.semaphore_signal(
        barrier, inc=1, device_id={"rows": peer(d)}, device_id_type=MESH))
    pl.semaphore_wait(barrier, groups + sides - 2)

    def copy_y(src, dst, send, recv, to):
        return pltpu.make_async_remote_copy(
            src_ref=src, dst_ref=dst, send_sem=send, recv_sem=recv,
            device_id={"cols": to}, device_id_type=MESH)

    def to_right(c):
        return copy_y(panel.at[pl.ds(c * chunk, chunk)], held.at[y * own + c],
                      send_r.at[c], recv_l.at[c], right)

    def to_left(c):
        return copy_y(panel.at[pl.ds(c * chunk, chunk)], held.at[y * own + c],
                      send_l.at[c], recv_r.at[c], left)

    def from_left(c):
        return copy_y(held.at[left * own + c], held.at[left * own + c],
                      send_r.at[c], recv_l.at[c], right)

    def from_right(c):
        return copy_y(held.at[right * own + c], held.at[right * own + c],
                      send_l.at[c], recv_r.at[c], left)

    def pass_right(c):
        return copy_y(held.at[left * own + c], held.at[left * own + c],
                      pass_send_r.at[c], pass_recv_l.at[c], right)

    def pass_left(c):
        return copy_y(held.at[right * own + half + c], held.at[right * own + half + c],
                      pass_send_l.at[c], pass_recv_r.at[c], left)

    def passed_left(c):
        return copy_y(held.at[across * own + c], held.at[across * own + c],
                      pass_send_r.at[c], pass_recv_l.at[c], right)

    def passed_right(c):
        return copy_y(held.at[across * own + half + c], held.at[across * own + half + c],
                      pass_send_l.at[c], pass_recv_r.at[c], left)

    def send_own(c):
        to_right(c).start()
        to_left(lax.rem(c + half, own)).start()

    loop(early, send_own)

    gram[...] = jnp.zeros_like(gram)
    both[...] = jnp.zeros_like(both)

    def gram_step(c):
        load_panel(c).wait()
        at = y * own + c
        x = held[at]
        x_high, x_low = split(x)
        high[at] = x_high
        low[at] = x_low
        x_turned = x.T.astype(jnp.bfloat16)
        gram[...] += dot(x_turned, x_high)
        both[:width, :] += dot(x_turned, x_low)

    loop(own, gram_step)
    mixed = both[:width, :]
    gram[...] += mixed + mixed.T

    def spread(src_of, dst, stage):
        def one(d):
            to = peer(d)
            pltpu.make_async_remote_copy(
                src_ref=src_of(to), dst_ref=dst.at[me],
                send_sem=small_send.at[stage], recv_sem=small_recv.at[stage],
                device_id={"rows": to}, device_id_type=MESH).start()

        loop(groups - 1, one)

    def spread_wait(dst, stage):
        some = dst.at[pl.ds(0, groups - 1)]
        everything = pltpu.make_async_remote_copy(
            src_ref=some, dst_ref=some,
            send_sem=small_send.at[stage], recv_sem=small_recv.at[stage],
            device_id={"rows": peer(0)}, device_id_type=MESH)
        everything.wait()

    spread(lambda to: gram.at[pl.ds(pl.multiple_of(to * part, 8), part)], gram_in, 0)
    gram_in[me] = gram[pl.ds(pl.multiple_of(me * part, 8), part), :]

    def turn(c):
        load_trail(c).wait()
        t_high, t_low = split(trail[c].T)
        turned[c, :columns, :] = t_high
        turned[c, columns:, :] = t_low

    loop(chunks, turn)
    spread_wait(gram_in, 0)
    gram_y[y] = jnp.sum(gram_in[...], axis=0)

    def over_y(d):
        return copy_y(gram_y.at[y], gram_y.at[y], small_send.at[1], small_recv.at[1], side(d))

    loop(sides - 1, lambda d: over_y(d).start())
    loop(own - early, lambda c: send_own(early + c))

    acc[...] = jnp.zeros_like(acc)

    def add_cross(at):
        product = dot(turned[at], high[at])
        acc[...] += product[:columns] + (
            product[columns:] + dot(turned[at, :columns, :], low[at]))

    loop(own, lambda c: add_cross(y * own + c))

    some = gram_y.at[pl.ds(0, sides - 1)]
    copy_y(some, some, small_send.at[1], small_recv.at[1], right).wait()
    gram_all[me] = jnp.sum(gram_y[...], axis=0)
    spread(lambda to: gram_all.at[me], gram_all, 2)
    spread_wait(gram_all, 2)

    row_at = lax.broadcasted_iota(jnp.int32, (width, width), 0)
    col_at = lax.broadcasted_iota(jnp.int32, (width, width), 1)
    work[:, :width] = gram_all[...].reshape(width, width)
    work[:, width:] = jnp.where(row_at == col_at, 1.0, 0.0)
    factor(work, width)
    r_factor[...] = jnp.where(row_at <= col_at, work[:, :width], 0.0)
    inverse = work[:, width:]
    both[:width, :] = inverse
    both[width:, :] = exact(inverse, inverse, ((0,), (0,)))

    def take(at):
        x_high, x_low = split(held[at])
        high[at] = x_high
        low[at] = x_low
        add_cross(at)

    def first_half(c):
        from_left(c).wait_recv()
        pass_right(c).start()
        from_right(half + c).wait_recv()
        pass_left(c).start()
        take(left * own + c)
        take(right * own + half + c)

    def second_half(c):
        from_left(half + c).wait_recv()
        take(left * own + half + c)
        from_right(c).wait_recv()
        take(right * own + c)

    def passed(c):
        passed_left(c).wait_recv()
        take(across * own + c)
        passed_right(c).wait_recv()
        take(across * own + half + c)

    loop(half, first_half)
    loop(half, second_half)
    loop(half, passed)

    for side_at in range(width // 128):
        cross_out[pl.ds(side_at * columns, columns), :] = acc[:, side_at * 128 : side_at * 128 + 128]
    spread(lambda to: cross_out.at[pl.ds(pl.multiple_of(to * part, 8), part)], cross_in, 3)
    cross_in[me] = cross_out[pl.ds(pl.multiple_of(me * part, 8), part), :]
    spread_wait(cross_in, 3)
    cross_all[me] = jnp.sum(cross_in[...], axis=0)
    spread(lambda to: cross_all.at[me], cross_all, 4)
    spread_wait(cross_all, 4)

    flat = cross_all[...].reshape(width, columns)
    cross = jnp.concatenate([flat[:columns], flat[columns:]], axis=1)
    solved = exact(both[...], cross, ((1,), (1,)))
    r_cross[...] = solved[:width]
    coeff[...] = solved[width:]

    def finish(c):
        to_right(c).wait_send()
        to_left(c).wait_send()

    loop(own, finish)

    def finish_passed(c):
        pass_right(c).wait_send()
        pass_left(c).wait_send()

    loop(half, finish_passed)


def residual_kernel(
    r_factor_in, r_cross_in, coeff, trail, high, low, r_factor, r_cross, residual, staged, out_sem
):
    chunks, chunk, columns = trail.shape
    c_high, c_low = split(coeff[...])
    c_both = jnp.concatenate([c_high, c_low], axis=1)

    def store(c):
        return pltpu.make_async_copy(
            staged.at[c], residual.at[pl.ds(c * chunk, chunk)], out_sem.at[c]
        )

    def project(c):
        product = dot(high[c], c_both)
        rest = product[:, columns:] + dot(low[c], c_high)
        staged[c] = trail[c] - (product[:, :columns] + rest)
        store(c).start()

    loop(chunks, project)
    r_factor[...] = r_factor_in[...]
    r_cross[...] = r_cross_in[...]
    loop(chunks, lambda c: store(c).wait())


def per_device(groups, chunk, panel, trailing):
    rows, width = panel.shape
    total, columns = trailing.shape
    own, chunks, part = rows // chunk, total // chunk, width // groups
    half = own // 2
    sides = total // rows
    f32, bf16 = jnp.float32, jnp.bfloat16
    dma = pltpu.SemaphoreType.DMA
    hbm = pl.BlockSpec(memory_space=pl.ANY)
    vmem = pl.BlockSpec(memory_space=pltpu.VMEM)
    r_factor, r_cross, coeff, trail, high, low = pl.pallas_call(
        functools.partial(kernel, groups, chunk),
        out_shape=(
            pltpu.VMEM((width, width), f32),
            pltpu.VMEM((width, columns), f32),
            pltpu.VMEM((width, columns), f32),
            pltpu.VMEM((chunks, chunk, columns), f32),
            pltpu.VMEM((chunks, chunk, width), bf16),
            pltpu.VMEM((chunks, chunk, width), bf16),
        ),
        in_specs=[hbm] * 2,
        out_specs=(vmem,) * 6,
        scratch_shapes=[
            pltpu.VMEM((chunks, chunk, width), f32),
            pltpu.VMEM((chunks, 2 * columns, chunk), bf16),
            pltpu.VMEM((width, width), f32),
            pltpu.VMEM((groups, part, width), f32),
            pltpu.VMEM((sides, part, width), f32),
            pltpu.VMEM((groups, part, width), f32),
            pltpu.VMEM((width, 2 * width), f32),
            pltpu.VMEM((2 * width, width), f32),
            pltpu.VMEM((columns, width), f32),
            pltpu.VMEM((width, columns), f32),
            pltpu.VMEM((groups, part, columns), f32),
            pltpu.VMEM((groups, part, columns), f32),
            dma((own,)), dma((chunks,)),
            dma((own,)), dma((own,)), dma((own,)), dma((own,)),
            dma((half,)), dma((half,)), dma((half,)), dma((half,)),
            dma((5,)), dma((5,)),
        ],
        compiler_params=pltpu.CompilerParams(
            collective_id=0, has_side_effects=True, vmem_limit_bytes=30 * 2**20
        ),
    )(panel, trailing)
    return pl.pallas_call(
        residual_kernel,
        out_shape=(
            jax.ShapeDtypeStruct((width, width), f32),
            jax.ShapeDtypeStruct((width, columns), f32),
            jax.ShapeDtypeStruct((total, columns), f32),
        ),
        in_specs=[vmem] * 6,
        out_specs=(vmem, vmem, hbm),
        scratch_shapes=[pltpu.VMEM((chunks, chunk, columns), f32), dma((chunks,))],
        compiler_params=pltpu.CompilerParams(vmem_limit_bytes=10 * 2**20),
    )(r_factor, r_cross, coeff, trail, high, low)


def solution(mesh):
    return jax.shard_map(
        functools.partial(per_device, mesh.shape["rows"], 512),
        mesh=mesh,
        in_specs=(P(("rows", "cols"), None), P("rows", "cols")),
        out_specs=(P(), P(None, "cols"), P("rows", "cols")),
        check_vma=False,
    )
```

```python
import functools
import math

import jax
import jax.numpy as jnp
from jax import lax
from jax.experimental import pallas as pl
from jax.experimental.pallas import tpu as pltpu
from jax.sharding import PartitionSpec as P

MESH = pl.DeviceIdType.MESH
BLOCK = 32


def split(x):
    high = x.astype(jnp.bfloat16)
    return high, (x - high.astype(jnp.float32)).astype(jnp.bfloat16)


def dot(a, b):
    return jnp.dot(a, b, preferred_element_type=jnp.float32)


def dot_turned(a, b):
    return lax.dot_general(a, b, (((1,), (1,)), ((), ())), preferred_element_type=jnp.float32)


def exact(a, b, dims):
    return lax.dot_general(
        a, b, (dims, ((), ())), precision=lax.Precision.HIGHEST, preferred_element_type=jnp.float32
    )


def loop(n, body):
    def step(i, carry):
        body(i)
        return carry

    lax.fori_loop(0, n, step, 0)


def factor(work, width):
    def block_step(k, carry):
        first = pl.multiple_of(k * BLOCK, BLOCK)
        rows = work[pl.ds(first, BLOCK), :]
        row_at = lax.broadcasted_iota(jnp.int32, (BLOCK, 1), 0)
        lane_at = lax.broadcasted_iota(jnp.int32, (BLOCK, width), 1)
        for j in range(BLOCK):
            column = jnp.sum(
                jnp.where(lane_at == first + j, rows[:, :width], 0.0), axis=1, keepdims=True
            )
            pivot = column[j : j + 1, :]
            scale = lax.rsqrt(pivot)
            scale = scale * (1.5 - 0.5 * pivot * scale * scale)
            pivot_row = rows[j : j + 1, :] * scale
            below = jnp.where(row_at > j, column * scale, 0.0)
            rows = jnp.where(row_at == j, pivot_row, rows - below * pivot_row)
        work[pl.ds(first, BLOCK), :] = rows
        later = jnp.where(lane_at >= first + BLOCK, rows[:, :width], 0.0)
        work[...] -= exact(later, rows, ((0,), (0,)))
        return carry

    lax.fori_loop(0, width // BLOCK, block_step, 0)


def kernel(
    groups, ring, chunk,
    panel, trailing, r_factor, r_cross, coeff, trail, high, low,
    held, turned, gram, gram_in, gram_y, gram_all, work, both, both_high, both_low,
    acc, cross_out, cross_in, cross_all,
    own_sem, trail_sem,
    send_r, send_l, recv_l, recv_r, pass_send_r, pass_send_l, pass_recv_l, pass_recv_r,
    small_send, small_recv, news,
):
    width = panel.shape[1]
    columns = trailing.shape[1]
    own = panel.shape[0] // chunk
    half = own // 2
    early = max(own * 3 // 8, 1)
    chunks = trailing.shape[0] // chunk
    part = width // groups
    me = lax.axis_index("rows")
    y = lax.axis_index("cols")
    sides = trailing.shape[0] // panel.shape[0]
    right = lax.rem(y + 1, sides)
    left = lax.rem(y + sides - 1, sides)
    across = lax.rem(y + 2, sides)

    def load_panel(c):
        return pltpu.make_async_copy(
            panel.at[pl.ds(c * chunk, chunk)], held.at[y * own + c], own_sem.at[c]
        )

    def load_trail(c):
        return pltpu.make_async_copy(
            trailing.at[pl.ds(c * chunk, chunk)], trail.at[c], trail_sem.at[c]
        )

    loop(own, lambda c: load_panel(c).start())
    loop(chunks, lambda c: load_trail(c).start())

    core, z, x = lax.rem(me, 2), lax.rem(me // 2, ring), me // (2 * ring)

    def at_xz(dx, dz, other):
        return (lax.rem(x + dx, ring) * ring + lax.rem(z + dz, ring)) * 2 + lax.rem(core + other, 2)

    def peer(i):
        return at_xz(ring // 2 + i // (2 * ring), ring // 2 + lax.rem(i // 2, ring), lax.rem(i, 2))

    itself = (ring - ring // 2) * (2 * ring + 2)

    def each_peer(body):
        loop(itself, lambda i: body(peer(i)))
        loop(groups - 1 - itself, lambda i: body(peer(itself + 1 + i)))

    def side(d):
        return lax.rem(y + d + 1, sides)

    def tell(sem, **to):
        pl.semaphore_signal(sem, inc=1, device_id=to, device_id_type=MESH)

    def tell_x(sem):
        tell(sem, rows=at_xz(1, 0, 0))
        tell(sem, rows=at_xz(ring - 1, 0, 0))

    def tell_y(sem):
        tell(sem, cols=right)
        tell(sem, cols=left)

    def tell_z(sem):
        tell(sem, rows=at_xz(0, 1, 0))
        tell(sem, rows=at_xz(0, ring - 1, 0))

    barrier = pltpu.get_barrier_semaphore()
    tell_y(barrier)
    tell_x(barrier)
    tell_z(barrier)
    tell(barrier, rows=at_xz(0, 0, 1))
    pl.semaphore_wait(barrier, 7)
    tell_x(news.at[0])
    tell_y(news.at[1])

    def copy_y(src, dst, send, recv, to):
        return pltpu.make_async_remote_copy(
            src_ref=src, dst_ref=dst, send_sem=send, recv_sem=recv,
            device_id={"cols": to}, device_id_type=MESH)

    def to_right(c):
        return copy_y(panel.at[pl.ds(c * chunk, chunk)], held.at[y * own + c],
                      send_r.at[c], recv_l.at[c], right)

    def to_left(c):
        return copy_y(panel.at[pl.ds(c * chunk, chunk)], held.at[y * own + c],
                      send_l.at[c], recv_r.at[c], left)

    def from_left(c):
        return copy_y(held.at[left * own + c], held.at[left * own + c],
                      send_r.at[c], recv_l.at[c], right)

    def from_right(c):
        return copy_y(held.at[right * own + c], held.at[right * own + c],
                      send_l.at[c], recv_r.at[c], left)

    def pass_right(c):
        return copy_y(held.at[left * own + c], held.at[left * own + c],
                      pass_send_r.at[c], pass_recv_l.at[c], right)

    def pass_left(c):
        return copy_y(held.at[right * own + half + c], held.at[right * own + half + c],
                      pass_send_l.at[c], pass_recv_r.at[c], left)

    def passed_left(c):
        return copy_y(held.at[across * own + c], held.at[across * own + c],
                      pass_send_r.at[c], pass_recv_l.at[c], right)

    def passed_right(c):
        return copy_y(held.at[across * own + half + c], held.at[across * own + half + c],
                      pass_send_l.at[c], pass_recv_r.at[c], left)

    def send_own(c):
        to_right(c).start()
        to_left(lax.rem(c + half, own)).start()

    loop(early, send_own)

    gram[...] = jnp.zeros_like(gram)
    both[...] = jnp.zeros_like(both)

    def gram_step(c):
        load_panel(c).wait()
        at = y * own + c
        x = held[at]
        x_high, x_low = split(x)
        high[at] = x_high
        low[at] = x_low
        x_turned = x.T.astype(jnp.bfloat16)
        gram[...] += dot(x_turned, x_high)
        both[:width, :] += dot(x_turned, x_low)

    loop(own, gram_step)
    pl.semaphore_wait(news.at[0], 2)
    tell_z(news.at[2])
    mixed = both[:width, :]
    gram[...] += mixed + mixed.T

    def spread(src_of, dst, stage):
        def one(to):
            pltpu.make_async_remote_copy(
                src_ref=src_of(to), dst_ref=dst.at[me],
                send_sem=small_send.at[stage], recv_sem=small_recv.at[stage],
                device_id={"rows": to}, device_id_type=MESH).start()

        each_peer(one)

    def spread_wait(dst, stage):
        some = dst.at[pl.ds(0, groups - 1)]
        everything = pltpu.make_async_remote_copy(
            src_ref=some, dst_ref=some,
            send_sem=small_send.at[stage], recv_sem=small_recv.at[stage],
            device_id={"rows": at_xz(1, 0, 0)}, device_id_type=MESH)
        everything.wait()

    def turn(c):
        load_trail(c).wait()
        t_high, t_low = split(trail[c].T)
        turned[c, :columns, :] = t_high
        turned[c, columns:, :] = t_low

    third = chunks // 3
    loop(third, turn)
    pl.semaphore_wait(news.at[2], 2)
    tell_z(news.at[3])
    loop(third, lambda c: turn(third + c))
    pl.semaphore_wait(news.at[3], 2)
    tell(news.at[4], rows=at_xz(0, 0, 1))
    loop(chunks - 2 * third, lambda c: turn(2 * third + c))
    pl.semaphore_wait(news.at[4], 1)
    pl.semaphore_wait(news.at[1], 2)

    spread(lambda to: gram.at[pl.ds(pl.multiple_of(to * part, 8), part)], gram_in, 0)
    gram_in[me] = gram[pl.ds(pl.multiple_of(me * part, 8), part), :]

    spread_wait(gram_in, 0)
    gram_y[y] = jnp.sum(gram_in[...], axis=0)

    def over_y(d):
        return copy_y(gram_y.at[y], gram_y.at[y], small_send.at[1], small_recv.at[1], side(d))

    loop(sides - 1, lambda d: over_y(d).start())
    loop(own - early, lambda c: send_own(early + c))

    acc[...] = jnp.zeros_like(acc)

    def add_cross(at):
        product = dot(turned[at], high[at])
        acc[...] += product[:columns] + (
            product[columns:] + dot(turned[at, :columns, :], low[at]))

    loop(own, lambda c: add_cross(y * own + c))

    some = gram_y.at[pl.ds(0, sides - 1)]
    copy_y(some, some, small_send.at[1], small_recv.at[1], right).wait()
    gram_all[me] = jnp.sum(gram_y[...], axis=0)
    spread(lambda to: gram_all.at[me], gram_all, 2)
    spread_wait(gram_all, 2)

    row_at = lax.broadcasted_iota(jnp.int32, (width, width), 0)
    col_at = lax.broadcasted_iota(jnp.int32, (width, width), 1)
    work[:, :width] = gram_all[...].reshape(width, width)
    work[:, width:] = jnp.where(row_at == col_at, 1.0, 0.0)
    factor(work, width)
    r_factor[...] = jnp.where(row_at <= col_at, work[:, :width], 0.0)
    inverse = work[:, width:]
    both[:width, :] = inverse
    both[width:, :] = exact(inverse, inverse, ((0,), (0,)))
    both_high[...], both_low[...] = split(both[...])

    def take(at):
        x_high, x_low = split(held[at])
        high[at] = x_high
        low[at] = x_low
        add_cross(at)

    def first_half(c):
        from_left(c).wait_recv()
        pass_right(c).start()
        from_right(half + c).wait_recv()
        pass_left(c).start()
        take(left * own + c)
        take(right * own + half + c)

    def second_half(c):
        from_left(half + c).wait_recv()
        take(left * own + half + c)
        from_right(c).wait_recv()
        take(right * own + c)

    def passed(c):
        passed_left(c).wait_recv()
        take(across * own + c)
        passed_right(c).wait_recv()
        take(across * own + half + c)

    loop(half, first_half)
    loop(half, second_half)
    loop(half, passed)

    for side_at in range(width // 128):
        cross_out[pl.ds(side_at * columns, columns), :] = acc[:, side_at * 128 : side_at * 128 + 128]
    spread(lambda to: cross_out.at[pl.ds(pl.multiple_of(to * part, 8), part)], cross_in, 3)
    cross_in[me] = cross_out[pl.ds(pl.multiple_of(me * part, 8), part), :]
    spread_wait(cross_in, 3)
    cross_all[me] = jnp.sum(cross_in[...], axis=0)
    spread(lambda to: cross_all.at[me], cross_all, 4)
    spread_wait(cross_all, 4)

    flat = cross_all[...].reshape(width, columns)
    cross = jnp.concatenate([flat[:columns], flat[columns:]], axis=1)
    x_high, x_low = split(cross)
    product = dot_turned(both_high[...], jnp.concatenate([x_high, x_low], axis=0))
    rest = product[:, columns:] + dot_turned(both_low[...], x_high)
    solved = product[:, :columns] + rest
    r_cross[...] = solved[:width]
    coeff[...] = solved[width:]

    def finish(c):
        to_right(c).wait_send()
        to_left(c).wait_send()

    loop(own, finish)

    def finish_passed(c):
        pass_right(c).wait_send()
        pass_left(c).wait_send()

    loop(half, finish_passed)


def residual_kernel(
    r_factor_in, r_cross_in, coeff, trail, high, low, r_factor, r_cross, residual, staged, out_sem
):
    chunks, chunk, columns = trail.shape
    c_high, c_low = split(coeff[...])
    c_both = jnp.concatenate([c_high, c_low], axis=1)

    steps, rows = chunks // 2, 2 * chunk

    def store(c):
        return pltpu.make_async_copy(
            staged.at[c], residual.at[pl.ds(c * rows, rows)], out_sem.at[c]
        )

    def some(ref, c):
        return ref[2 * c : 2 * c + 2].reshape(rows, ref.shape[2])

    for c in range(steps):
        product = dot(some(high, c), c_both)
        rest = product[:, columns:] + dot(some(low, c), c_high)
        staged[c] = some(trail, c) - (product[:, :columns] + rest)
        store(c).start()
    r_factor[...] = r_factor_in[...]
    r_cross[...] = r_cross_in[...]
    loop(steps, lambda c: store(c).wait())


def per_device(groups, chunk, panel, trailing):
    ring = math.isqrt(groups // 2)
    rows, width = panel.shape
    total, columns = trailing.shape
    own, chunks, part = rows // chunk, total // chunk, width // groups
    half = own // 2
    sides = total // rows
    f32, bf16 = jnp.float32, jnp.bfloat16
    dma = pltpu.SemaphoreType.DMA
    hbm = pl.BlockSpec(memory_space=pl.ANY)
    vmem = pl.BlockSpec(memory_space=pltpu.VMEM)
    r_factor, r_cross, coeff, trail, high, low = pl.pallas_call(
        functools.partial(kernel, groups, ring, chunk),
        out_shape=(
            pltpu.VMEM((width, width), f32),
            pltpu.VMEM((width, columns), f32),
            pltpu.VMEM((width, columns), f32),
            pltpu.VMEM((chunks, chunk, columns), f32),
            pltpu.VMEM((chunks, chunk, width), bf16),
            pltpu.VMEM((chunks, chunk, width), bf16),
        ),
        in_specs=[hbm] * 2,
        out_specs=(vmem,) * 6,
        scratch_shapes=[
            pltpu.VMEM((chunks, chunk, width), f32),
            pltpu.VMEM((chunks, 2 * columns, chunk), bf16),
            pltpu.VMEM((width, width), f32),
            pltpu.VMEM((groups, part, width), f32),
            pltpu.VMEM((sides, part, width), f32),
            pltpu.VMEM((groups, part, width), f32),
            pltpu.VMEM((width, 2 * width), f32),
            pltpu.VMEM((2 * width, width), f32),
            pltpu.VMEM((2 * width, width), bf16),
            pltpu.VMEM((2 * width, width), bf16),
            pltpu.VMEM((columns, width), f32),
            pltpu.VMEM((width, columns), f32),
            pltpu.VMEM((groups, part, columns), f32),
            pltpu.VMEM((groups, part, columns), f32),
            dma((own,)), dma((chunks,)),
            dma((own,)), dma((own,)), dma((own,)), dma((own,)),
            dma((half,)), dma((half,)), dma((half,)), dma((half,)),
            dma((5,)), dma((5,)), pltpu.SemaphoreType.REGULAR((5,)),
        ],
        compiler_params=pltpu.CompilerParams(
            collective_id=0, has_side_effects=True, vmem_limit_bytes=30 * 2**20
        ),
    )(panel, trailing)
    return pl.pallas_call(
        residual_kernel,
        out_shape=(
            jax.ShapeDtypeStruct((width, width), f32),
            jax.ShapeDtypeStruct((width, columns), f32),
            jax.ShapeDtypeStruct((total, columns), f32),
        ),
        in_specs=[vmem] * 6,
        out_specs=(vmem, vmem, hbm),
        scratch_shapes=[pltpu.VMEM((chunks // 2, 2 * chunk, columns), f32), dma((chunks // 2,))],
        compiler_params=pltpu.CompilerParams(vmem_limit_bytes=10 * 2**20),
    )(r_factor, r_cross, coeff, trail, high, low)


def solution(mesh):
    return jax.shard_map(
        functools.partial(per_device, mesh.shape["rows"], 512),
        mesh=mesh,
        in_specs=(P(("rows", "cols"), None), P("rows", "cols")),
        out_specs=(P(), P(None, "cols"), P("rows", "cols")),
        check_vma=False,
    )
```

```python
import functools
import math

import jax
import jax.numpy as jnp
from jax import lax
from jax.experimental import pallas as pl
from jax.experimental.pallas import tpu as pltpu
from jax.sharding import PartitionSpec as P

MESH = pl.DeviceIdType.MESH
CHUNK = 512
LATE = 1
STEPS = 16
BLOCK = 32


def split(x):
    high = x.astype(jnp.bfloat16)
    return high, (x - high.astype(jnp.float32)).astype(jnp.bfloat16)


def dot(a, b):
    return jnp.dot(a, b, preferred_element_type=jnp.float32)


def dot_turned(a, b):
    return lax.dot_general(a, b, (((1,), (1,)), ((), ())), preferred_element_type=jnp.float32)


def exact(a, b, dims):
    return lax.dot_general(
        a, b, (dims, ((), ())), precision=lax.Precision.HIGHEST, preferred_element_type=jnp.float32
    )


def loop(n, body):
    def step(i, carry):
        body(i)
        return carry

    lax.fori_loop(0, n, step, 0)


def factor(work, width):
    def block_step(k, carry):
        first = pl.multiple_of(k * BLOCK, BLOCK)
        rows = work[pl.ds(first, BLOCK), :]
        row_at = lax.broadcasted_iota(jnp.int32, (BLOCK, 1), 0)
        lane_at = lax.broadcasted_iota(jnp.int32, (BLOCK, width), 1)
        for j in range(BLOCK):
            column = jnp.sum(
                jnp.where(lane_at == first + j, rows[:, :width], 0.0), axis=1, keepdims=True
            )
            pivot = column[j : j + 1, :]
            scale = lax.rsqrt(pivot)
            scale = scale * (1.5 - 0.5 * pivot * scale * scale)
            pivot_row = rows[j : j + 1, :] * scale
            below = jnp.where(row_at > j, column * scale, 0.0)
            rows = jnp.where(row_at == j, pivot_row, rows - below * pivot_row)
        work[pl.ds(first, BLOCK), :] = rows
        later = jnp.where(lane_at >= first + BLOCK, rows[:, :width], 0.0)
        work[...] -= exact(later, rows, ((0,), (0,)))
        return carry

    lax.fori_loop(0, width // BLOCK, block_step, 0)


def kernel(
    groups, ring, chunk, late,
    panel, trailing, r_factor, r_cross, coeff, trail, high, low,
    held, turned, gram, gram_in, gram_y, gram_all, work, both, both_high, both_low,
    acc, cross_out, cross_in, cross_all, guest, guest_out, guest_in, guest_sum, guest_part,
    own_sem, trail_sem,
    send_r, send_l, recv_l, recv_r, pass_send_r, pass_send_l, pass_recv_l, pass_recv_r,
    small_send, small_recv, guest_send, guest_recv, part_send, part_recv, news,
):
    width = panel.shape[1]
    columns = trailing.shape[1]
    own = panel.shape[0] // chunk
    half = own // 2
    early = max(own * 3 // 8, 1)
    chunks = trailing.shape[0] // chunk
    part = width // groups
    me = lax.axis_index("rows")
    y = lax.axis_index("cols")
    sides = trailing.shape[0] // panel.shape[0]
    right = lax.rem(y + 1, sides)
    left = lax.rem(y + sides - 1, sides)
    across = lax.rem(y + 2, sides)

    def load_panel(c):
        return pltpu.make_async_copy(
            panel.at[pl.ds(c * chunk, chunk)], held.at[y * own + c], own_sem.at[c]
        )

    def load_trail(c):
        return pltpu.make_async_copy(
            trailing.at[pl.ds(c * chunk, chunk)], trail.at[c], trail_sem.at[c]
        )

    loop(own, lambda c: load_panel(c).start())
    loop(chunks, lambda c: load_trail(c).start())

    core, z, x = lax.rem(me, 2), lax.rem(me // 2, ring), me // (2 * ring)

    def at_xz(dx, dz, other):
        return (lax.rem(x + dx, ring) * ring + lax.rem(z + dz, ring)) * 2 + lax.rem(core + other, 2)

    def peer(i):
        return at_xz(ring // 2 + i // (2 * ring), ring // 2 + lax.rem(i // 2, ring), lax.rem(i, 2))

    itself = (ring - ring // 2) * (2 * ring + 2)

    def each_peer(body):
        loop(itself, lambda i: body(peer(i)))
        loop(groups - 1 - itself, lambda i: body(peer(itself + 1 + i)))

    def side(d):
        return lax.rem(y + d + 1, sides)

    def tell(sem, **to):
        pl.semaphore_signal(sem, inc=1, device_id=to, device_id_type=MESH)

    def tell_x(sem):
        tell(sem, rows=at_xz(1, 0, 0))
        tell(sem, rows=at_xz(ring - 1, 0, 0))

    def tell_y(sem):
        tell(sem, cols=right)
        tell(sem, cols=left)

    def tell_z(sem):
        tell(sem, rows=at_xz(0, 1, 0))
        tell(sem, rows=at_xz(0, ring - 1, 0))

    barrier = pltpu.get_barrier_semaphore()
    tell_y(barrier)
    tell_x(barrier)
    tell_z(barrier)
    tell(barrier, rows=at_xz(0, 0, 1))
    pl.semaphore_wait(barrier, 7)
    tell_x(news.at[0])
    tell_y(news.at[1])

    def copy_y(src, dst, send, recv, to):
        return pltpu.make_async_remote_copy(
            src_ref=src, dst_ref=dst, send_sem=send, recv_sem=recv,
            device_id={"cols": to}, device_id_type=MESH)

    def to_right(c):
        return copy_y(panel.at[pl.ds(c * chunk, chunk)], held.at[y * own + c],
                      send_r.at[c], recv_l.at[c], right)

    def to_left(c):
        return copy_y(panel.at[pl.ds(c * chunk, chunk)], held.at[y * own + c],
                      send_l.at[c], recv_r.at[c], left)

    def from_left(c):
        return copy_y(held.at[left * own + c], held.at[left * own + c],
                      send_r.at[c], recv_l.at[c], right)

    def from_right(c):
        return copy_y(held.at[right * own + c], held.at[right * own + c],
                      send_l.at[c], recv_r.at[c], left)

    def pass_right(c):
        return copy_y(held.at[left * own + c], held.at[left * own + c],
                      pass_send_r.at[c], pass_recv_l.at[c], right)

    def pass_left(c):
        return copy_y(held.at[right * own + half + c], held.at[right * own + half + c],
                      pass_send_l.at[c], pass_recv_r.at[c], left)

    def passed_left(c):
        return copy_y(held.at[across * own + c], held.at[across * own + c],
                      pass_send_r.at[c], pass_recv_l.at[c], right)

    def passed_right(c):
        return copy_y(held.at[across * own + half + c], held.at[across * own + half + c],
                      pass_send_l.at[c], pass_recv_r.at[c], left)

    def guest_left():
        rows = trailing.at[pl.ds((across * own + half - late) * chunk, late * chunk)]
        return copy_y(rows, guest.at[0], guest_send.at[0], guest_recv.at[0], left)

    def guest_right():
        rows = trailing.at[pl.ds((across * own + own - late) * chunk, late * chunk)]
        return copy_y(rows, guest.at[1], guest_send.at[1], guest_recv.at[1], right)

    def part_right():
        return copy_y(guest_sum.at[0], guest_part.at[0], part_send.at[0], part_recv.at[0], right)

    def part_left():
        return copy_y(guest_sum.at[1], guest_part.at[1], part_send.at[1], part_recv.at[1], left)

    def send_own(c):
        to_right(c).start()
        to_left(lax.rem(c + half, own)).start()

    loop(early, send_own)

    gram[...] = jnp.zeros_like(gram)
    both[...] = jnp.zeros_like(both)

    def gram_step(c):
        load_panel(c).wait()
        at = y * own + c
        x = held[at]
        x_high, x_low = split(x)
        high[at] = x_high
        low[at] = x_low
        x_turned = x.T.astype(jnp.bfloat16)
        gram[...] += dot(x_turned, x_high)
        both[:width, :] += dot(x_turned, x_low)

    loop(own, gram_step)
    pl.semaphore_wait(news.at[0], 2)
    tell_z(news.at[2])
    mixed = both[:width, :]
    gram[...] += mixed + mixed.T

    def spread(src_of, dst, stage):
        def one(to):
            pltpu.make_async_remote_copy(
                src_ref=src_of(to), dst_ref=dst.at[me],
                send_sem=small_send.at[stage], recv_sem=small_recv.at[stage],
                device_id={"rows": to}, device_id_type=MESH).start()

        each_peer(one)

    def spread_wait(dst, stage):
        some = dst.at[pl.ds(0, groups - 1)]
        everything = pltpu.make_async_remote_copy(
            src_ref=some, dst_ref=some,
            send_sem=small_send.at[stage], recv_sem=small_recv.at[stage],
            device_id={"rows": at_xz(1, 0, 0)}, device_id_type=MESH)
        everything.wait()

    def turn(c):
        load_trail(c).wait()
        t_high, t_low = split(trail[c].T)
        turned[c, :columns, :] = t_high
        turned[c, columns:, :] = t_low

    third = chunks // 3
    loop(third, turn)
    pl.semaphore_wait(news.at[2], 2)
    tell_z(news.at[3])
    loop(third, lambda c: turn(third + c))
    pl.semaphore_wait(news.at[3], 2)
    tell(news.at[4], rows=at_xz(0, 0, 1))
    loop(chunks - 2 * third, lambda c: turn(2 * third + c))
    pl.semaphore_wait(news.at[4], 1)
    pl.semaphore_wait(news.at[1], 2)

    spread(lambda to: gram.at[pl.ds(pl.multiple_of(to * part, 8), part)], gram_in, 0)
    gram_in[me] = gram[pl.ds(pl.multiple_of(me * part, 8), part), :]

    spread_wait(gram_in, 0)
    gram_y[y] = jnp.sum(gram_in[...], axis=0)

    def over_y(d):
        return copy_y(gram_y.at[y], gram_y.at[y], small_send.at[1], small_recv.at[1], side(d))

    loop(sides - 1, lambda d: over_y(d).start())
    guest_left().start()
    guest_right().start()
    loop(own - early, lambda c: send_own(early + c))

    acc[...] = jnp.zeros_like(acc)

    def cross_of(t_both, at):
        x_high, x_low = (
            ref[pl.ds(at, t_both.shape[1] // chunk)].reshape(t_both.shape[1], width)
            for ref in (high, low))
        product = dot(t_both, x_high)
        return product[:columns] + (product[columns:] + dot(t_both[:columns], x_low))

    def add_cross(at):
        acc[...] += cross_of(turned[at], at)

    def lay(out, first, sums):
        for side_at in range(width // 128):
            out[pl.ds(side_at * columns, columns), first : first + columns] = (
                sums[:, side_at * 128 : side_at * 128 + 128])

    def mine(ref):
        return ref[pl.ds(pl.multiple_of(me * part, 8), part), :]

    def slice_for(ref):
        return lambda to: ref.at[pl.ds(pl.multiple_of(to * part, 8), part)]

    loop(own, lambda c: add_cross(y * own + c))

    some = gram_y.at[pl.ds(0, sides - 1)]
    copy_y(some, some, small_send.at[1], small_recv.at[1], right).wait()
    gram_all[me] = jnp.sum(gram_y[...], axis=0)
    spread(lambda to: gram_all.at[me], gram_all, 2)
    spread_wait(gram_all, 2)

    row_at = lax.broadcasted_iota(jnp.int32, (width, width), 0)
    col_at = lax.broadcasted_iota(jnp.int32, (width, width), 1)
    work[:, :width] = gram_all[...].reshape(width, width)
    work[:, width:] = jnp.where(row_at == col_at, 1.0, 0.0)
    factor(work, width)
    r_factor[...] = jnp.where(row_at <= col_at, work[:, :width], 0.0)
    inverse = work[:, width:]
    both[:width, :] = inverse
    both[width:, :] = exact(inverse, inverse, ((0,), (0,)))
    both_high[...], both_low[...] = split(both[...])

    def take(at):
        x_high, x_low = split(held[at])
        high[at] = x_high
        low[at] = x_low
        add_cross(at)

    def first_half(c):
        from_left(c).wait_recv()
        pass_right(c).start()
        from_right(half + c).wait_recv()
        pass_left(c).start()
        take(left * own + c)
        take(right * own + half + c)

    def guests():
        for c in range(half - late, half):
            from_left(c).wait_recv()
            take(left * own + c)
            from_right(half + c).wait_recv()
            take(right * own + half + c)
        for place, at in ((0, left * own + half - late), (1, right * own + own - late)):
            copy_y(guest.at[place], guest.at[place],
                   guest_send.at[place], guest_recv.at[place], right).wait_recv()
            t_both = jnp.concatenate(split(guest[place].T), axis=0)
            lay(guest_out, place * columns, cross_of(t_both, at))
        spread(slice_for(guest_out), guest_in, 5)
        guest_in[me] = mine(guest_out)

    def second_half(c):
        from_left(half + c).wait_recv()
        take(left * own + half + c)
        from_right(c).wait_recv()
        take(right * own + c)

    def passed(c):
        passed_left(c).wait_recv()
        take(across * own + c)
        passed_right(c).wait_recv()
        take(across * own + half + c)

    loop(half - late, first_half)
    guests()
    loop(half, second_half)
    spread_wait(guest_in, 5)
    sums = jnp.sum(guest_in[...], axis=0)
    guest_sum[0] = sums[:, :columns]
    guest_sum[1] = sums[:, columns:]
    part_right().start()
    part_left().start()
    for c in range(half - late, half):
        pass_right(c).start()
        pass_left(c).start()
    loop(half - late, passed)

    lay(cross_out, 0, acc[...])
    spread(slice_for(cross_out), cross_in, 3)
    cross_in[me] = mine(cross_out)
    for place in range(2):
        copy_y(guest_part.at[place], guest_part.at[place],
               part_send.at[place], part_recv.at[place], right).wait_recv()
    spread_wait(cross_in, 3)
    cross_all[me] = jnp.sum(cross_in[...], axis=0) + (guest_part[0] + guest_part[1])
    spread(lambda to: cross_all.at[me], cross_all, 4)
    spread_wait(cross_all, 4)

    flat = cross_all[...].reshape(width, columns)
    cross = jnp.concatenate([flat[:columns], flat[columns:]], axis=1)
    x_high, x_low = split(cross)
    product = dot_turned(both_high[...], jnp.concatenate([x_high, x_low], axis=0))
    rest = product[:, columns:] + dot_turned(both_low[...], x_high)
    solved = product[:, :columns] + rest
    r_cross[...] = solved[:width]
    coeff[...] = solved[width:]

    def keep(at):
        high[at], low[at] = split(held[at])

    for c in range(half - late, half):
        passed_left(c).wait_recv()
        keep(across * own + c)
        passed_right(c).wait_recv()
        keep(across * own + half + c)

    def finish(c):
        to_right(c).wait_send()
        to_left(c).wait_send()

    loop(own, finish)

    def finish_passed(c):
        pass_right(c).wait_send()
        pass_left(c).wait_send()

    loop(half, finish_passed)
    for copy in (guest_left(), guest_right(), part_right(), part_left()):
        copy.wait_send()


def residual_kernel(
    r_factor_in, r_cross_in, coeff, trail, high, low, r_factor, r_cross, residual, staged, out_sem
):
    chunks, chunk, columns = trail.shape
    c_high, c_low = split(coeff[...])
    c_both = jnp.concatenate([c_high, c_low], axis=1)

    steps, rows = STEPS, chunks * chunk // STEPS
    each = chunks // steps

    def store(c):
        return pltpu.make_async_copy(
            staged.at[c], residual.at[pl.ds(c * rows, rows)], out_sem.at[c]
        )

    def some(ref, c):
        return ref[each * c : each * (c + 1)].reshape(rows, ref.shape[2])

    for c in range(steps):
        product = dot(some(high, c), c_both)
        rest = product[:, columns:] + dot(some(low, c), c_high)
        staged[c] = some(trail, c) - (product[:, :columns] + rest)
        store(c).start()
    r_factor[...] = r_factor_in[...]
    r_cross[...] = r_cross_in[...]
    loop(steps, lambda c: store(c).wait())


def per_device(groups, chunk, late, panel, trailing):
    ring = math.isqrt(groups // 2)
    rows, width = panel.shape
    total, columns = trailing.shape
    own, chunks, part = rows // chunk, total // chunk, width // groups
    half = own // 2
    sides = total // rows
    f32, bf16 = jnp.float32, jnp.bfloat16
    dma = pltpu.SemaphoreType.DMA
    hbm = pl.BlockSpec(memory_space=pl.ANY)
    vmem = pl.BlockSpec(memory_space=pltpu.VMEM)
    r_factor, r_cross, coeff, trail, high, low = pl.pallas_call(
        functools.partial(kernel, groups, ring, chunk, late),
        out_shape=(
            pltpu.VMEM((width, width), f32),
            pltpu.VMEM((width, columns), f32),
            pltpu.VMEM((width, columns), f32),
            pltpu.VMEM((chunks, chunk, columns), f32),
            pltpu.VMEM((chunks, chunk, width), bf16),
            pltpu.VMEM((chunks, chunk, width), bf16),
        ),
        in_specs=[hbm] * 2,
        out_specs=(vmem,) * 6,
        scratch_shapes=[
            pltpu.VMEM((chunks, chunk, width), f32),
            pltpu.VMEM((chunks, 2 * columns, chunk), bf16),
            pltpu.VMEM((width, width), f32),
            pltpu.VMEM((groups, part, width), f32),
            pltpu.VMEM((sides, part, width), f32),
            pltpu.VMEM((groups, part, width), f32),
            pltpu.VMEM((width, 2 * width), f32),
            pltpu.VMEM((2 * width, width), f32),
            pltpu.VMEM((2 * width, width), bf16),
            pltpu.VMEM((2 * width, width), bf16),
            pltpu.VMEM((columns, width), f32),
            pltpu.VMEM((width, columns), f32),
            pltpu.VMEM((groups, part, columns), f32),
            pltpu.VMEM((groups, part, columns), f32),
            pltpu.VMEM((2, late * chunk, columns), f32),
            pltpu.VMEM((width, 2 * columns), f32),
            pltpu.VMEM((groups, part, 2 * columns), f32),
            pltpu.VMEM((2, part, columns), f32),
            pltpu.VMEM((2, part, columns), f32),
            dma((own,)), dma((chunks,)),
            dma((own,)), dma((own,)), dma((own,)), dma((own,)),
            dma((half,)), dma((half,)), dma((half,)), dma((half,)),
            dma((6,)), dma((6,)), dma((2,)), dma((2,)), dma((2,)), dma((2,)), pltpu.SemaphoreType.REGULAR((5,)),
        ],
        compiler_params=pltpu.CompilerParams(
            collective_id=0, has_side_effects=True, vmem_limit_bytes=30 * 2**20
        ),
    )(panel, trailing)
    return pl.pallas_call(
        residual_kernel,
        out_shape=(
            jax.ShapeDtypeStruct((width, width), f32),
            jax.ShapeDtypeStruct((width, columns), f32),
            jax.ShapeDtypeStruct((total, columns), f32),
        ),
        in_specs=[vmem] * 6,
        out_specs=(vmem, vmem, hbm),
        scratch_shapes=[pltpu.VMEM((STEPS, total // STEPS, columns), f32), dma((STEPS,))],
        compiler_params=pltpu.CompilerParams(vmem_limit_bytes=10 * 2**20),
    )(r_factor, r_cross, coeff, trail, high, low)


def solution(mesh):
    return jax.shard_map(
        functools.partial(per_device, mesh.shape["rows"], CHUNK, LATE),
        mesh=mesh,
        in_specs=(P(("rows", "cols"), None), P("rows", "cols")),
        out_specs=(P(), P(None, "cols"), P("rows", "cols")),
        check_vma=False,
    )
```

```python
import functools
import math

import jax
import jax.numpy as jnp
from jax import lax
from jax.experimental import pallas as pl
from jax.experimental.pallas import tpu as pltpu
from jax.sharding import PartitionSpec as P

MESH = pl.DeviceIdType.MESH
CHUNK = 256
LATE = 3
STEPS = 16
BLOCK = 32


def split(x):
    high = x.astype(jnp.bfloat16)
    return high, (x - high.astype(jnp.float32)).astype(jnp.bfloat16)


def dot(a, b):
    return jnp.dot(a, b, preferred_element_type=jnp.float32)


def dot_turned(a, b):
    return lax.dot_general(a, b, (((1,), (1,)), ((), ())), preferred_element_type=jnp.float32)


def exact(a, b, dims):
    return lax.dot_general(
        a, b, (dims, ((), ())), precision=lax.Precision.HIGHEST, preferred_element_type=jnp.float32
    )


def loop(n, body):
    def step(i, carry):
        body(i)
        return carry

    lax.fori_loop(0, n, step, 0)


def split_coeff(coeff):
    high, low = split(coeff)
    return high, jnp.concatenate([high, low], axis=1)


def project(weights, trail, high, low, c):
    chunks, chunk, columns = trail.shape
    each = chunks // STEPS

    def some(ref):
        return ref[each * c : each * (c + 1)].reshape(each * chunk, ref.shape[2])

    c_high, c_both = weights
    product = dot(some(high), c_both)
    rest = product[:, columns:] + dot(some(low), c_high)
    return (some(trail) - (product[:, :columns] + rest)).reshape(each, chunk, columns)


def whole(c):
    return c % 2 == 0


def factor(work, width):
    def block_step(k, carry):
        first = pl.multiple_of(k * BLOCK, BLOCK)
        rows = work[pl.ds(first, BLOCK), :]
        row_at = lax.broadcasted_iota(jnp.int32, (BLOCK, 1), 0)
        lane_at = lax.broadcasted_iota(jnp.int32, (BLOCK, width), 1)
        for j in range(BLOCK):
            column = jnp.sum(
                jnp.where(lane_at == first + j, rows[:, :width], 0.0), axis=1, keepdims=True
            )
            pivot = column[j : j + 1, :]
            scale = lax.rsqrt(pivot)
            scale = scale * (1.5 - 0.5 * pivot * scale * scale)
            pivot_row = rows[j : j + 1, :] * scale
            below = jnp.where(row_at > j, column * scale, 0.0)
            rows = jnp.where(row_at == j, pivot_row, rows - below * pivot_row)
        work[pl.ds(first, BLOCK), :] = rows
        later = jnp.where(lane_at >= first + BLOCK, rows[:, :width], 0.0)
        work[...] -= exact(later, rows, ((0,), (0,)))
        return carry

    lax.fori_loop(0, width // BLOCK, block_step, 0)


def kernel(
    groups, ring, chunk, late,
    panel, trailing, r_factor, r_cross, coeff, trail, high, low,
    held, turned, gram, gram_in, gram_y, gram_all, work, both, both_high, both_low,
    acc, cross_out, cross_in, cross_all, guest, guest_out, guest_in, guest_sum, guest_part,
    own_sem, trail_sem,
    send_r, send_l, recv_l, recv_r, pass_send_r, pass_send_l, pass_recv_l, pass_recv_r,
    small_send, small_recv, guest_send, guest_recv, part_send, part_recv, news,
):
    width = panel.shape[1]
    columns = trailing.shape[1]
    own = panel.shape[0] // chunk
    half = own // 2
    early = max(own * 3 // 8, 1)
    chunks = trailing.shape[0] // chunk
    part = width // groups
    me = lax.axis_index("rows")
    y = lax.axis_index("cols")
    sides = trailing.shape[0] // panel.shape[0]
    right = lax.rem(y + 1, sides)
    left = lax.rem(y + sides - 1, sides)
    across = lax.rem(y + 2, sides)

    def load_panel(c):
        return pltpu.make_async_copy(
            panel.at[pl.ds(c * chunk, chunk)], held.at[y * own + c], own_sem.at[c]
        )

    def load_trail(c):
        return pltpu.make_async_copy(
            trailing.at[pl.ds(c * chunk, chunk)], trail.at[c], trail_sem.at[c]
        )

    core, z, x = lax.rem(me, 2), lax.rem(me // 2, ring), me // (2 * ring)

    def at_xz(dx, dz, other):
        return (lax.rem(x + dx, ring) * ring + lax.rem(z + dz, ring)) * 2 + lax.rem(core + other, 2)

    def peer(i):
        return at_xz(ring // 2 + i // (2 * ring), ring // 2 + lax.rem(i // 2, ring), lax.rem(i, 2))

    itself = (ring - ring // 2) * (2 * ring + 2)

    def each_peer(body):
        loop(itself, lambda i: body(peer(i)))
        loop(groups - 1 - itself, lambda i: body(peer(itself + 1 + i)))

    def side(d):
        return lax.rem(y + d + 1, sides)

    def tell(sem, **to):
        pl.semaphore_signal(sem, inc=1, device_id=to, device_id_type=MESH)

    def tell_x(sem):
        tell(sem, rows=at_xz(1, 0, 0))
        tell(sem, rows=at_xz(ring - 1, 0, 0))

    def tell_y(sem):
        tell(sem, cols=right)
        tell(sem, cols=left)

    def tell_z(sem):
        tell(sem, rows=at_xz(0, 1, 0))
        tell(sem, rows=at_xz(0, ring - 1, 0))

    barrier = pltpu.get_barrier_semaphore()
    tell_y(barrier)
    tell_x(barrier)
    tell_z(barrier)
    tell(barrier, rows=at_xz(0, 0, 1))
    loop(own, lambda c: load_panel(c).start())
    pl.semaphore_wait(barrier, 7)
    tell_x(news.at[0])
    tell_y(news.at[1])

    def copy_y(src, dst, send, recv, to):
        return pltpu.make_async_remote_copy(
            src_ref=src, dst_ref=dst, send_sem=send, recv_sem=recv,
            device_id={"cols": to}, device_id_type=MESH)

    def to_right(c):
        return copy_y(panel.at[pl.ds(c * chunk, chunk)], held.at[y * own + c],
                      send_r.at[c], recv_l.at[c], right)

    def to_left(c):
        return copy_y(panel.at[pl.ds(c * chunk, chunk)], held.at[y * own + c],
                      send_l.at[c], recv_r.at[c], left)

    def from_left(c):
        return copy_y(held.at[left * own + c], held.at[left * own + c],
                      send_r.at[c], recv_l.at[c], right)

    def from_right(c):
        return copy_y(held.at[right * own + c], held.at[right * own + c],
                      send_l.at[c], recv_r.at[c], left)

    def pass_right(c):
        return copy_y(held.at[left * own + c], held.at[left * own + c],
                      pass_send_r.at[c], pass_recv_l.at[c], right)

    def pass_left(c):
        return copy_y(held.at[right * own + half + c], held.at[right * own + half + c],
                      pass_send_l.at[c], pass_recv_r.at[c], left)

    def passed_left(c):
        return copy_y(held.at[across * own + c], held.at[across * own + c],
                      pass_send_r.at[c], pass_recv_l.at[c], right)

    def passed_right(c):
        return copy_y(held.at[across * own + half + c], held.at[across * own + half + c],
                      pass_send_l.at[c], pass_recv_r.at[c], left)

    def guest_left():
        rows = trailing.at[pl.ds((across * own + half - late) * chunk, late * chunk)]
        return copy_y(rows, guest.at[0], guest_send.at[0], guest_recv.at[0], left)

    def guest_right():
        rows = trailing.at[pl.ds((across * own + own - late) * chunk, late * chunk)]
        return copy_y(rows, guest.at[1], guest_send.at[1], guest_recv.at[1], right)

    def part_right():
        return copy_y(guest_sum.at[0], guest_part.at[0], part_send.at[0], part_recv.at[0], right)

    def part_left():
        return copy_y(guest_sum.at[1], guest_part.at[1], part_send.at[1], part_recv.at[1], left)

    def send_own(c):
        to_right(c).start()
        to_left(lax.rem(c + half, own)).start()

    loop(early, send_own)
    loop(chunks, lambda c: load_trail(c).start())

    gram[...] = jnp.zeros_like(gram)
    both[...] = jnp.zeros_like(both)

    def gram_step(c):
        load_panel(c).wait()
        at = y * own + c
        x = held[at]
        x_high, x_low = split(x)
        high[at] = x_high
        low[at] = x_low
        x_turned = x.T.astype(jnp.bfloat16)
        gram[...] += dot(x_turned, x_high)
        both[:width, :] += dot(x_turned, x_low)

    loop(own, gram_step)
    pl.semaphore_wait(news.at[0], 2)
    tell_z(news.at[2])
    mixed = both[:width, :]
    gram[...] += mixed + mixed.T

    def spread(src_of, dst, stage):
        def one(to):
            pltpu.make_async_remote_copy(
                src_ref=src_of(to), dst_ref=dst.at[me],
                send_sem=small_send.at[stage], recv_sem=small_recv.at[stage],
                device_id={"rows": to}, device_id_type=MESH).start()

        each_peer(one)

    def spread_wait(dst, stage):
        some = dst.at[pl.ds(0, groups - 1)]
        everything = pltpu.make_async_remote_copy(
            src_ref=some, dst_ref=some,
            send_sem=small_send.at[stage], recv_sem=small_recv.at[stage],
            device_id={"rows": at_xz(1, 0, 0)}, device_id_type=MESH)
        everything.wait()

    def turn(c):
        load_trail(c).wait()
        t_high, t_low = split(trail[c].T)
        turned[c, :columns, :] = t_high
        turned[c, columns:, :] = t_low

    third = chunks // 3
    loop(third, turn)
    pl.semaphore_wait(news.at[2], 2)
    tell_z(news.at[3])
    loop(third, lambda c: turn(third + c))
    pl.semaphore_wait(news.at[3], 2)
    tell(news.at[4], rows=at_xz(0, 0, 1))
    loop(chunks - 2 * third, lambda c: turn(2 * third + c))
    pl.semaphore_wait(news.at[4], 1)
    pl.semaphore_wait(news.at[1], 2)

    spread(lambda to: gram.at[pl.ds(pl.multiple_of(to * part, 8), part)], gram_in, 0)
    gram_in[me] = gram[pl.ds(pl.multiple_of(me * part, 8), part), :]

    spread_wait(gram_in, 0)
    gram_y[y] = jnp.sum(gram_in[...], axis=0)

    def over_y(d):
        return copy_y(gram_y.at[y], gram_y.at[y], small_send.at[1], small_recv.at[1], side(d))

    loop(sides - 1, lambda d: over_y(d).start())
    guest_left().start()
    guest_right().start()
    loop(own - early, lambda c: send_own(early + c))

    acc[...] = jnp.zeros_like(acc)

    def cross_of(t_both, at):
        x_high, x_low = (
            ref[pl.ds(at, t_both.shape[1] // chunk)].reshape(t_both.shape[1], width)
            for ref in (high, low))
        product = dot(t_both, x_high)
        return product[:columns] + (product[columns:] + dot(t_both[:columns], x_low))

    def add_cross(at):
        acc[...] += cross_of(turned[at], at)

    def lay(out, first, sums):
        for side_at in range(width // 128):
            out[pl.ds(side_at * columns, columns), first : first + columns] = (
                sums[:, side_at * 128 : side_at * 128 + 128])

    def mine(ref):
        return ref[pl.ds(pl.multiple_of(me * part, 8), part), :]

    def slice_for(ref):
        return lambda to: ref.at[pl.ds(pl.multiple_of(to * part, 8), part)]

    loop(own, lambda c: add_cross(y * own + c))

    some = gram_y.at[pl.ds(0, sides - 1)]
    copy_y(some, some, small_send.at[1], small_recv.at[1], right).wait()
    gram_all[me] = jnp.sum(gram_y[...], axis=0)
    spread(lambda to: gram_all.at[me], gram_all, 2)
    spread_wait(gram_all, 2)

    row_at = lax.broadcasted_iota(jnp.int32, (width, width), 0)
    col_at = lax.broadcasted_iota(jnp.int32, (width, width), 1)
    work[:, :width] = gram_all[...].reshape(width, width)
    work[:, width:] = jnp.where(row_at == col_at, 1.0, 0.0)
    factor(work, width)
    r_factor[...] = jnp.where(row_at <= col_at, work[:, :width], 0.0)
    inverse = work[:, width:]
    both[:width, :] = inverse
    both[width:, :] = exact(inverse, inverse, ((0,), (0,)))
    both_high[...], both_low[...] = split(both[...])

    def take(at):
        x_high, x_low = split(held[at])
        high[at] = x_high
        low[at] = x_low
        add_cross(at)

    def first_half(c):
        from_left(c).wait_recv()
        pass_right(c).start()
        from_right(half + c).wait_recv()
        pass_left(c).start()
        take(left * own + c)
        take(right * own + half + c)

    def guests():
        for c in range(half - late, half):
            from_left(c).wait_recv()
            take(left * own + c)
            from_right(half + c).wait_recv()
            take(right * own + half + c)
        for place, at in ((0, left * own + half - late), (1, right * own + own - late)):
            copy_y(guest.at[place], guest.at[place],
                   guest_send.at[place], guest_recv.at[place], right).wait_recv()
            t_both = jnp.concatenate(split(guest[place].T), axis=0)
            lay(guest_out, place * columns, cross_of(t_both, at))
        spread(slice_for(guest_out), guest_in, 5)
        guest_in[me] = mine(guest_out)

    def second_half(c):
        from_left(half + c).wait_recv()
        take(left * own + half + c)
        from_right(c).wait_recv()
        take(right * own + c)

    def passed(c):
        passed_left(c).wait_recv()
        take(across * own + c)
        passed_right(c).wait_recv()
        take(across * own + half + c)

    loop(half - late, first_half)
    guests()
    loop(half, second_half)
    spread_wait(guest_in, 5)
    sums = jnp.sum(guest_in[...], axis=0)
    guest_sum[0] = sums[:, :columns]
    guest_sum[1] = sums[:, columns:]
    part_right().start()
    part_left().start()
    for c in range(half - late, half):
        pass_right(c).start()
        pass_left(c).start()

    def finish(c):
        to_right(c).wait_send()
        to_left(c).wait_send()

    loop(own, finish)
    for copy in (guest_left(), guest_right()):
        copy.wait_send()
    loop(half - late, passed)

    lay(cross_out, 0, acc[...])
    spread(slice_for(cross_out), cross_in, 3)
    cross_in[me] = mine(cross_out)
    for place in range(2):
        copy_y(guest_part.at[place], guest_part.at[place],
               part_send.at[place], part_recv.at[place], right).wait_recv()
    spread_wait(cross_in, 3)
    cross_all[me] = jnp.sum(cross_in[...], axis=0) + (guest_part[0] + guest_part[1])
    spread(lambda to: cross_all.at[me], cross_all, 4)

    def finish_passed(c):
        pass_right(c).wait_send()
        pass_left(c).wait_send()

    loop(half - late, finish_passed)
    for copy in (part_right(), part_left()):
        copy.wait_send()
    spread_wait(cross_all, 4)

    flat = cross_all[...].reshape(width, columns)
    cross = jnp.concatenate([flat[:columns], flat[columns:]], axis=1)
    x_high, x_low = split(cross)
    product = dot_turned(both_high[...], jnp.concatenate([x_high, x_low], axis=0))
    rest = product[:, columns:] + dot_turned(both_low[...], x_high)
    solved = product[:, :columns] + rest
    r_cross[...] = solved[:width]
    coeff[...] = solved[width:]
    weights = split_coeff(solved[width:])
    each = chunks // STEPS
    for c in range(STEPS):
        if whole(c):
            trail[each * c : each * (c + 1)] = project(weights, trail, high, low, c)

    def keep(at):
        high[at], low[at] = split(held[at])

    for c in range(half - late, half):
        passed_left(c).wait_recv()
        keep(across * own + c)
        passed_right(c).wait_recv()
        keep(across * own + half + c)

    loop(late, lambda c: finish_passed(half - late + c))


def residual_kernel(
    r_factor_in, r_cross_in, coeff, trail, high, low, r_factor, r_cross, residual, staged, out_sem
):
    each = trail.shape[0] // STEPS

    def store(c, rows):
        return pltpu.make_async_copy(
            rows, residual.at[pl.ds(each * c, each)], out_sem.at[c]
        )

    def rows_of(c):
        return trail.at[pl.ds(each * c, each)] if whole(c) else staged.at[c // 2]

    for c in range(STEPS):
        if whole(c):
            store(c, rows_of(c)).start()
    weights = split_coeff(coeff[...])
    for c in range(STEPS):
        if not whole(c):
            staged[c // 2] = project(weights, trail, high, low, c)
            store(c, rows_of(c)).start()
    r_factor[...] = r_factor_in[...]
    r_cross[...] = r_cross_in[...]
    for c in range(STEPS):
        store(c, rows_of(c)).wait()


def per_device(groups, chunk, late, panel, trailing):
    ring = math.isqrt(groups // 2)
    rows, width = panel.shape
    total, columns = trailing.shape
    own, chunks, part = rows // chunk, total // chunk, width // groups
    half = own // 2
    sides = total // rows
    f32, bf16 = jnp.float32, jnp.bfloat16
    dma = pltpu.SemaphoreType.DMA
    hbm = pl.BlockSpec(memory_space=pl.ANY)
    vmem = pl.BlockSpec(memory_space=pltpu.VMEM)
    r_factor, r_cross, coeff, trail, high, low = pl.pallas_call(
        functools.partial(kernel, groups, ring, chunk, late),
        out_shape=(
            pltpu.VMEM((width, width), f32),
            pltpu.VMEM((width, columns), f32),
            pltpu.VMEM((width, columns), f32),
            pltpu.VMEM((chunks, chunk, columns), f32),
            pltpu.VMEM((chunks, chunk, width), bf16),
            pltpu.VMEM((chunks, chunk, width), bf16),
        ),
        in_specs=[hbm] * 2,
        out_specs=(vmem,) * 6,
        scratch_shapes=[
            pltpu.VMEM((chunks, chunk, width), f32),
            pltpu.VMEM((chunks, 2 * columns, chunk), bf16),
            pltpu.VMEM((width, width), f32),
            pltpu.VMEM((groups, part, width), f32),
            pltpu.VMEM((sides, part, width), f32),
            pltpu.VMEM((groups, part, width), f32),
            pltpu.VMEM((width, 2 * width), f32),
            pltpu.VMEM((2 * width, width), f32),
            pltpu.VMEM((2 * width, width), bf16),
            pltpu.VMEM((2 * width, width), bf16),
            pltpu.VMEM((columns, width), f32),
            pltpu.VMEM((width, columns), f32),
            pltpu.VMEM((groups, part, columns), f32),
            pltpu.VMEM((groups, part, columns), f32),
            pltpu.VMEM((2, late * chunk, columns), f32),
            pltpu.VMEM((width, 2 * columns), f32),
            pltpu.VMEM((groups, part, 2 * columns), f32),
            pltpu.VMEM((2, part, columns), f32),
            pltpu.VMEM((2, part, columns), f32),
            dma((own,)), dma((chunks,)),
            dma((own,)), dma((own,)), dma((own,)), dma((own,)),
            dma((half,)), dma((half,)), dma((half,)), dma((half,)),
            dma((6,)), dma((6,)), dma((2,)), dma((2,)), dma((2,)), dma((2,)), pltpu.SemaphoreType.REGULAR((5,)),
        ],
        compiler_params=pltpu.CompilerParams(
            collective_id=0, has_side_effects=True, vmem_limit_bytes=30 * 2**20
        ),
    )(panel, trailing)
    r_factor, r_cross, residual = pl.pallas_call(
        residual_kernel,
        out_shape=(
            jax.ShapeDtypeStruct((width, width), f32),
            jax.ShapeDtypeStruct((width, columns), f32),
            jax.ShapeDtypeStruct((chunks, chunk, columns), f32),
        ),
        in_specs=[vmem] * 6,
        out_specs=(vmem, vmem, hbm),
        scratch_shapes=[pltpu.VMEM((STEPS // 2, chunks // STEPS, chunk, columns), f32), dma((STEPS,))],
        compiler_params=pltpu.CompilerParams(vmem_limit_bytes=10 * 2**20),
    )(r_factor, r_cross, coeff, trail, high, low)
    return r_factor, r_cross, residual.reshape(total, columns)


def solution(mesh):
    return jax.shard_map(
        functools.partial(per_device, mesh.shape["rows"], CHUNK, LATE),
        mesh=mesh,
        in_specs=(P(("rows", "cols"), None), P("rows", "cols")),
        out_specs=(P(), P(None, "cols"), P("rows", "cols")),
        check_vma=False,
    )
```

```python
import functools
import math

import jax
import jax.numpy as jnp
from jax import lax
from jax.experimental import pallas as pl
from jax.experimental.pallas import tpu as pltpu
from jax.sharding import PartitionSpec as P

MESH = pl.DeviceIdType.MESH
CHUNK = 512
LATE = 1
STEPS = 16
BLOCK = 32


def split(x):
    high = x.astype(jnp.bfloat16)
    return high, (x - high.astype(jnp.float32)).astype(jnp.bfloat16)


def dot(a, b):
    return jnp.dot(a, b, preferred_element_type=jnp.float32)


def dot_turned(a, b):
    return lax.dot_general(a, b, (((1,), (1,)), ((), ())), preferred_element_type=jnp.float32)


def exact(a, b, dims):
    return lax.dot_general(
        a, b, (dims, ((), ())), precision=lax.Precision.HIGHEST, preferred_element_type=jnp.float32
    )


def loop(n, body):
    def step(i, carry):
        body(i)
        return carry

    lax.fori_loop(0, n, step, 0)


def split_coeff(coeff):
    high, low = split(coeff)
    return high, jnp.concatenate([high, low], axis=1)


def project(weights, trail, high, low, c):
    chunks, chunk, columns = trail.shape
    each = chunks // STEPS

    def some(ref):
        return ref[each * c : each * (c + 1)].reshape(each * chunk, ref.shape[2])

    c_high, c_both = weights
    product = dot(some(high), c_both)
    rest = product[:, columns:] + dot(some(low), c_high)
    return (some(trail) - (product[:, :columns] + rest)).reshape(each, chunk, columns)


def whole(c):
    return c % 2 == 0


def factor(work, width):
    def block_step(k, carry):
        first = pl.multiple_of(k * BLOCK, BLOCK)
        rows = work[pl.ds(first, BLOCK), :]
        row_at = lax.broadcasted_iota(jnp.int32, (BLOCK, 1), 0)
        lane_at = lax.broadcasted_iota(jnp.int32, (BLOCK, width), 1)
        for j in range(BLOCK):
            column = jnp.sum(
                jnp.where(lane_at == first + j, rows[:, :width], 0.0), axis=1, keepdims=True
            )
            pivot = column[j : j + 1, :]
            scale = lax.rsqrt(pivot)
            scale = scale * (1.5 - 0.5 * pivot * scale * scale)
            pivot_row = rows[j : j + 1, :] * scale
            below = jnp.where(row_at > j, column * scale, 0.0)
            rows = jnp.where(row_at == j, pivot_row, rows - below * pivot_row)
        work[pl.ds(first, BLOCK), :] = rows
        later = jnp.where(lane_at >= first + BLOCK, rows[:, :width], 0.0)
        work[...] -= exact(later, rows, ((0,), (0,)))
        return carry

    lax.fori_loop(0, width // BLOCK, block_step, 0)


def kernel(
    groups, ring, chunk, late,
    panel, trailing, r_factor, r_cross, coeff, trail, high, low,
    held, turned, gram, gram_in, gram_y, gram_all, work, both, both_high, both_low,
    acc, cross_out, cross_in, cross_all, guest, guest_out, guest_in, guest_sum, guest_part,
    own_sem, trail_sem,
    send_r, send_l, recv_l, recv_r, pass_send_r, pass_send_l, pass_recv_l, pass_recv_r,
    small_send, small_recv, guest_send, guest_recv, part_send, part_recv, news,
):
    width = panel.shape[1]
    columns = trailing.shape[1]
    own = panel.shape[0] // chunk
    half = own // 2
    early = max(own * 3 // 8, 1)
    chunks = trailing.shape[0] // chunk
    part = width // groups
    edge, cut = half - late - 1, chunk // 2
    late_rows = late * chunk + cut
    me = lax.axis_index("rows")
    y = lax.axis_index("cols")
    sides = trailing.shape[0] // panel.shape[0]
    right = lax.rem(y + 1, sides)
    left = lax.rem(y + sides - 1, sides)
    across = lax.rem(y + 2, sides)

    def load_panel(c):
        return pltpu.make_async_copy(
            panel.at[pl.ds(c * chunk, chunk)], held.at[y * own + c], own_sem.at[c]
        )

    def load_trail(c):
        return pltpu.make_async_copy(
            trailing.at[pl.ds(c * chunk, chunk)], trail.at[c], trail_sem.at[c]
        )

    core, z, x = lax.rem(me, 2), lax.rem(me // 2, ring), me // (2 * ring)

    def at_xz(dx, dz, other):
        return (lax.rem(x + dx, ring) * ring + lax.rem(z + dz, ring)) * 2 + lax.rem(core + other, 2)

    def peer(i):
        return at_xz(ring // 2 + i // (2 * ring), ring // 2 + lax.rem(i // 2, ring), lax.rem(i, 2))

    itself = (ring - ring // 2) * (2 * ring + 2)

    def each_peer(body):
        loop(itself, lambda i: body(peer(i)))
        loop(groups - 1 - itself, lambda i: body(peer(itself + 1 + i)))

    def side(d):
        return lax.rem(y + d + 1, sides)

    def tell(sem, **to):
        pl.semaphore_signal(sem, inc=1, device_id=to, device_id_type=MESH)

    def tell_x(sem):
        tell(sem, rows=at_xz(1, 0, 0))
        tell(sem, rows=at_xz(ring - 1, 0, 0))

    def tell_y(sem):
        tell(sem, cols=right)
        tell(sem, cols=left)

    def tell_z(sem):
        tell(sem, rows=at_xz(0, 1, 0))
        tell(sem, rows=at_xz(0, ring - 1, 0))

    barrier = pltpu.get_barrier_semaphore()
    tell_y(barrier)
    tell_x(barrier)
    tell_z(barrier)
    tell(barrier, rows=at_xz(0, 0, 1))
    loop(own, lambda c: load_panel(c).start())
    pl.semaphore_wait(barrier, 7)
    tell_x(news.at[0])
    tell_y(news.at[1])

    def copy_y(src, dst, send, recv, to):
        return pltpu.make_async_remote_copy(
            src_ref=src, dst_ref=dst, send_sem=send, recv_sem=recv,
            device_id={"cols": to}, device_id_type=MESH)

    def to_right(c):
        return copy_y(panel.at[pl.ds(c * chunk, chunk)], held.at[y * own + c],
                      send_r.at[c], recv_l.at[c], right)

    def to_left(c):
        return copy_y(panel.at[pl.ds(c * chunk, chunk)], held.at[y * own + c],
                      send_l.at[c], recv_r.at[c], left)

    def from_left(c):
        return copy_y(held.at[left * own + c], held.at[left * own + c],
                      send_r.at[c], recv_l.at[c], right)

    def from_right(c):
        return copy_y(held.at[right * own + c], held.at[right * own + c],
                      send_l.at[c], recv_r.at[c], left)

    def piece(at, c, rows):
        return held.at[at + c] if rows is None else held.at[at + c, pl.ds(rows * cut, cut)]

    def pass_right(c, rows=None):
        ref, sem = piece(left * own, c, rows), half if rows == 1 else c
        return copy_y(ref, ref, pass_send_r.at[sem], pass_recv_l.at[sem], right)

    def pass_left(c, rows=None):
        ref, sem = piece(right * own + half, c, rows), half if rows == 1 else c
        return copy_y(ref, ref, pass_send_l.at[sem], pass_recv_r.at[sem], left)

    def passed_left(c, rows=None):
        ref, sem = piece(across * own, c, rows), half if rows == 1 else c
        return copy_y(ref, ref, pass_send_r.at[sem], pass_recv_l.at[sem], right)

    def passed_right(c, rows=None):
        ref, sem = piece(across * own + half, c, rows), half if rows == 1 else c
        return copy_y(ref, ref, pass_send_l.at[sem], pass_recv_r.at[sem], left)

    def guest_left():
        rows = trailing.at[pl.ds((across * own + half) * chunk - late_rows, late_rows)]
        return copy_y(rows, guest.at[0], guest_send.at[0], guest_recv.at[0], left)

    def guest_right():
        rows = trailing.at[pl.ds((across * own + own) * chunk - late_rows, late_rows)]
        return copy_y(rows, guest.at[1], guest_send.at[1], guest_recv.at[1], right)

    def part_right():
        return copy_y(guest_sum.at[0], guest_part.at[0], part_send.at[0], part_recv.at[0], right)

    def part_left():
        return copy_y(guest_sum.at[1], guest_part.at[1], part_send.at[1], part_recv.at[1], left)

    def send_own(c):
        to_right(c).start()
        to_left(lax.rem(c + half, own)).start()

    loop(early, send_own)
    loop(chunks, lambda c: load_trail(c).start())

    gram[...] = jnp.zeros_like(gram)
    both[...] = jnp.zeros_like(both)

    def gram_step(c):
        load_panel(c).wait()
        at = y * own + c
        x = held[at]
        x_high, x_low = split(x)
        high[at] = x_high
        low[at] = x_low
        x_turned = x.T.astype(jnp.bfloat16)
        gram[...] += dot(x_turned, x_high)
        both[:width, :] += dot(x_turned, x_low)

    loop(own, gram_step)
    pl.semaphore_wait(news.at[0], 2)
    tell_z(news.at[2])
    mixed = both[:width, :]
    gram[...] += mixed + mixed.T

    def spread(src_of, dst, stage):
        def one(to):
            pltpu.make_async_remote_copy(
                src_ref=src_of(to), dst_ref=dst.at[me],
                send_sem=small_send.at[stage], recv_sem=small_recv.at[stage],
                device_id={"rows": to}, device_id_type=MESH).start()

        each_peer(one)

    def spread_wait(dst, stage):
        some = dst.at[pl.ds(0, groups - 1)]
        everything = pltpu.make_async_remote_copy(
            src_ref=some, dst_ref=some,
            send_sem=small_send.at[stage], recv_sem=small_recv.at[stage],
            device_id={"rows": at_xz(1, 0, 0)}, device_id_type=MESH)
        everything.wait()

    def turn(c):
        load_trail(c).wait()
        t_high, t_low = split(trail[c].T)
        turned[c, :columns, :] = t_high
        turned[c, columns:, :] = t_low

    third = chunks // 3
    loop(third, turn)
    pl.semaphore_wait(news.at[2], 2)
    tell_z(news.at[3])
    loop(third, lambda c: turn(third + c))
    pl.semaphore_wait(news.at[3], 2)
    tell(news.at[4], rows=at_xz(0, 0, 1))
    loop(chunks - 2 * third, lambda c: turn(2 * third + c))
    pl.semaphore_wait(news.at[4], 1)
    pl.semaphore_wait(news.at[1], 2)

    spread(lambda to: gram.at[pl.ds(pl.multiple_of(to * part, 8), part)], gram_in, 0)
    gram_in[me] = gram[pl.ds(pl.multiple_of(me * part, 8), part), :]

    spread_wait(gram_in, 0)
    gram_y[y] = jnp.sum(gram_in[...], axis=0)

    def over_y(d):
        return copy_y(gram_y.at[y], gram_y.at[y], small_send.at[1], small_recv.at[1], side(d))

    loop(sides - 1, lambda d: over_y(d).start())
    guest_left().start()
    guest_right().start()
    loop(own - early, lambda c: send_own(early + c))

    acc[...] = jnp.zeros_like(acc)

    def cross_of(t_both, x_high, x_low):
        product = dot(t_both, x_high)
        return product[:columns] + (product[columns:] + dot(t_both[:columns], x_low))

    def add_cross(at):
        acc[...] += cross_of(turned[at], high[at], low[at])

    def lay(out, first, sums):
        for side_at in range(width // 128):
            out[pl.ds(side_at * columns, columns), first : first + columns] = (
                sums[:, side_at * 128 : side_at * 128 + 128])

    def mine(ref):
        return ref[pl.ds(pl.multiple_of(me * part, 8), part), :]

    def slice_for(ref):
        return lambda to: ref.at[pl.ds(pl.multiple_of(to * part, 8), part)]

    loop(own, lambda c: add_cross(y * own + c))

    some = gram_y.at[pl.ds(0, sides - 1)]
    copy_y(some, some, small_send.at[1], small_recv.at[1], right).wait()
    gram_all[me] = jnp.sum(gram_y[...], axis=0)
    spread(lambda to: gram_all.at[me], gram_all, 2)
    spread_wait(gram_all, 2)

    row_at = lax.broadcasted_iota(jnp.int32, (width, width), 0)
    col_at = lax.broadcasted_iota(jnp.int32, (width, width), 1)
    work[:, :width] = gram_all[...].reshape(width, width)
    work[:, width:] = jnp.where(row_at == col_at, 1.0, 0.0)
    factor(work, width)
    r_factor[...] = jnp.where(row_at <= col_at, work[:, :width], 0.0)
    inverse = work[:, width:]
    both[:width, :] = inverse
    both[width:, :] = exact(inverse, inverse, ((0,), (0,)))
    both_high[...], both_low[...] = split(both[...])

    def take(at):
        x_high, x_low = split(held[at])
        high[at] = x_high
        low[at] = x_low
        add_cross(at)

    def first_half(c, rows=None):
        from_left(c).wait_recv()
        pass_right(c, rows).start()
        from_right(half + c).wait_recv()
        pass_left(c, rows).start()
        take(left * own + c)
        take(right * own + half + c)

    def guests():
        for c in range(half - late, half):
            from_left(c).wait_recv()
            take(left * own + c)
            from_right(half + c).wait_recv()
            take(right * own + half + c)
        for place, at in ((0, left * own + half), (1, right * own + own)):
            copy_y(guest.at[place], guest.at[place],
                   guest_send.at[place], guest_recv.at[place], right).wait_recv()
            t_both = jnp.concatenate(split(guest[place].T), axis=0)
            x_high, x_low = (
                jnp.concatenate([
                    ref[at - late - 1, chunk - cut :],
                    ref[pl.ds(at - late, late)].reshape(late * chunk, width),
                ], axis=0)
                for ref in (high, low))
            lay(guest_out, place * columns, cross_of(t_both, x_high, x_low))
        spread(slice_for(guest_out), guest_in, 5)
        guest_in[me] = mine(guest_out)

    def second_half(c):
        from_left(half + c).wait_recv()
        take(left * own + half + c)
        from_right(c).wait_recv()
        take(right * own + c)

    def keep_cut(at, rows):
        x_high, x_low = split(held[at, rows])
        high[at, rows] = x_high
        low[at, rows] = x_low
        return x_high, x_low

    def take_cut(at):
        x_high, x_low = keep_cut(at, slice(0, cut))
        acc[...] += cross_of(turned[at, :, :cut], x_high, x_low)

    def passed(c):
        passed_left(c).wait_recv()
        take(across * own + c)
        passed_right(c).wait_recv()
        take(across * own + half + c)

    loop(edge, first_half)
    first_half(edge, 0)
    guests()
    loop(half, second_half)
    spread_wait(guest_in, 5)
    sums = jnp.sum(guest_in[...], axis=0)
    guest_sum[0] = sums[:, :columns]
    guest_sum[1] = sums[:, columns:]
    part_right().start()
    part_left().start()
    pass_right(edge, 1).start()
    pass_left(edge, 1).start()
    for c in range(edge + 1, half):
        pass_right(c).start()
        pass_left(c).start()

    def finish(c):
        to_right(c).wait_send()
        to_left(c).wait_send()

    loop(own, finish)
    for copy in (guest_left(), guest_right()):
        copy.wait_send()
    loop(edge, passed)
    passed_left(edge, 0).wait_recv()
    take_cut(across * own + edge)
    passed_right(edge, 0).wait_recv()
    take_cut(across * own + half + edge)

    lay(cross_out, 0, acc[...])
    spread(slice_for(cross_out), cross_in, 3)
    cross_in[me] = mine(cross_out)
    for place in range(2):
        copy_y(guest_part.at[place], guest_part.at[place],
               part_send.at[place], part_recv.at[place], right).wait_recv()
    spread_wait(cross_in, 3)
    cross_all[me] = jnp.sum(cross_in[...], axis=0) + (guest_part[0] + guest_part[1])
    spread(lambda to: cross_all.at[me], cross_all, 4)

    def finish_passed(c, rows=None):
        pass_right(c, rows).wait_send()
        pass_left(c, rows).wait_send()

    loop(edge, finish_passed)
    finish_passed(edge, 0)
    for copy in (part_right(), part_left()):
        copy.wait_send()
    spread_wait(cross_all, 4)

    flat = cross_all[...].reshape(width, columns)
    cross = jnp.concatenate([flat[:columns], flat[columns:]], axis=1)
    x_high, x_low = split(cross)
    x_both = jnp.concatenate([x_high, x_low], axis=0)

    def solve(rows):
        product = dot_turned(both_high[rows, :], x_both)
        rest = product[:, columns:] + dot_turned(both_low[rows, :], x_high)
        return product[:, :columns] + rest

    solved = solve(slice(width, 2 * width))
    coeff[...] = solved
    weights = split_coeff(solved)
    each = chunks // STEPS
    for c in range(STEPS):
        if whole(c):
            trail[each * c : each * (c + 1)] = project(weights, trail, high, low, c)
    r_cross[...] = solve(slice(0, width))

    def keep(at):
        high[at], low[at] = split(held[at])

    passed_left(edge, 1).wait_recv()
    keep_cut(across * own + edge, slice(cut, chunk))
    passed_right(edge, 1).wait_recv()
    keep_cut(across * own + half + edge, slice(cut, chunk))
    for c in range(edge + 1, half):
        passed_left(c).wait_recv()
        keep(across * own + c)
        passed_right(c).wait_recv()
        keep(across * own + half + c)

    finish_passed(edge, 1)
    loop(late, lambda c: finish_passed(edge + 1 + c))


def residual_kernel(
    r_factor_in, r_cross_in, coeff, trail, high, low, r_factor, r_cross, residual, staged, out_sem, small_sem
):
    each = trail.shape[0] // STEPS

    def store(c, rows):
        return pltpu.make_async_copy(
            rows, residual.at[pl.ds(each * c, each)], out_sem.at[c]
        )

    def rows_of(c):
        return trail.at[pl.ds(each * c, each)] if whole(c) else staged.at[c // 2]

    small = (
        pltpu.make_async_copy(r_factor_in, r_factor, small_sem.at[0]),
        pltpu.make_async_copy(r_cross_in, r_cross, small_sem.at[1]),
    )
    for c in range(STEPS):
        if whole(c):
            store(c, rows_of(c)).start()
    for copy in small:
        copy.start()
    weights = split_coeff(coeff[...])
    for c in range(STEPS):
        if not whole(c):
            staged[c // 2] = project(weights, trail, high, low, c)
            store(c, rows_of(c)).start()
    for c in range(STEPS):
        store(c, rows_of(c)).wait()
    for copy in small:
        copy.wait()


def per_device(groups, chunk, late, panel, trailing):
    ring = math.isqrt(groups // 2)
    rows, width = panel.shape
    total, columns = trailing.shape
    own, chunks, part = rows // chunk, total // chunk, width // groups
    half = own // 2
    sides = total // rows
    f32, bf16 = jnp.float32, jnp.bfloat16
    dma = pltpu.SemaphoreType.DMA
    hbm = pl.BlockSpec(memory_space=pl.ANY)
    vmem = pl.BlockSpec(memory_space=pltpu.VMEM)
    r_factor, r_cross, coeff, trail, high, low = pl.pallas_call(
        functools.partial(kernel, groups, ring, chunk, late),
        out_shape=(
            pltpu.VMEM((width, width), f32),
            pltpu.VMEM((width, columns), f32),
            pltpu.VMEM((width, columns), f32),
            pltpu.VMEM((chunks, chunk, columns), f32),
            pltpu.VMEM((chunks, chunk, width), bf16),
            pltpu.VMEM((chunks, chunk, width), bf16),
        ),
        in_specs=[hbm] * 2,
        out_specs=(vmem,) * 6,
        scratch_shapes=[
            pltpu.VMEM((chunks, chunk, width), f32),
            pltpu.VMEM((chunks, 2 * columns, chunk), bf16),
            pltpu.VMEM((width, width), f32),
            pltpu.VMEM((groups, part, width), f32),
            pltpu.VMEM((sides, part, width), f32),
            pltpu.VMEM((groups, part, width), f32),
            pltpu.VMEM((width, 2 * width), f32),
            pltpu.VMEM((2 * width, width), f32),
            pltpu.VMEM((2 * width, width), bf16),
            pltpu.VMEM((2 * width, width), bf16),
            pltpu.VMEM((columns, width), f32),
            pltpu.VMEM((width, columns), f32),
            pltpu.VMEM((groups, part, columns), f32),
            pltpu.VMEM((groups, part, columns), f32),
            pltpu.VMEM((2, late * chunk + chunk // 2, columns), f32),
            pltpu.VMEM((width, 2 * columns), f32),
            pltpu.VMEM((groups, part, 2 * columns), f32),
            pltpu.VMEM((2, part, columns), f32),
            pltpu.VMEM((2, part, columns), f32),
            dma((own,)), dma((chunks,)),
            dma((own,)), dma((own,)), dma((own,)), dma((own,)),
            dma((half + 1,)), dma((half + 1,)), dma((half + 1,)), dma((half + 1,)),
            dma((6,)), dma((6,)), dma((2,)), dma((2,)), dma((2,)), dma((2,)), pltpu.SemaphoreType.REGULAR((5,)),
        ],
        compiler_params=pltpu.CompilerParams(
            collective_id=0, has_side_effects=True, vmem_limit_bytes=34 * 2**20
        ),
    )(panel, trailing)
    r_factor, r_cross, residual = pl.pallas_call(
        residual_kernel,
        out_shape=(
            jax.ShapeDtypeStruct((width, width), f32),
            jax.ShapeDtypeStruct((width, columns), f32),
            jax.ShapeDtypeStruct((chunks, chunk, columns), f32),
        ),
        in_specs=[vmem] * 6,
        out_specs=(hbm,) * 3,
        scratch_shapes=[pltpu.VMEM((STEPS // 2, chunks // STEPS, chunk, columns), f32), dma((STEPS,)), dma((2,))],
        compiler_params=pltpu.CompilerParams(vmem_limit_bytes=10 * 2**20),
    )(r_factor, r_cross, coeff, trail, high, low)
    return r_factor, r_cross, residual.reshape(total, columns)


def solution(mesh):
    return jax.shard_map(
        functools.partial(per_device, mesh.shape["rows"], CHUNK, LATE),
        mesh=mesh,
        in_specs=(P(("rows", "cols"), None), P("rows", "cols")),
        out_specs=(P(), P(None, "cols"), P("rows", "cols")),
        check_vma=False,
    )
```

```python
import functools
import math

import jax
import jax.numpy as jnp
from jax import lax
from jax.experimental import pallas as pl
from jax.experimental.pallas import tpu as pltpu
from jax.sharding import PartitionSpec as P

MESH = pl.DeviceIdType.MESH
CHUNK = 512
LATE = 1
STEPS = 16
BLOCK = 32


def split(x):
    high = x.astype(jnp.bfloat16)
    return high, (x - high.astype(jnp.float32)).astype(jnp.bfloat16)


def dot(a, b):
    return jnp.dot(a, b, preferred_element_type=jnp.float32)


def dot_turned(a, b):
    return lax.dot_general(a, b, (((1,), (1,)), ((), ())), preferred_element_type=jnp.float32)


def exact(a, b, dims):
    return lax.dot_general(
        a, b, (dims, ((), ())), precision=lax.Precision.HIGHEST, preferred_element_type=jnp.float32
    )


def loop(n, body):
    def step(i, carry):
        body(i)
        return carry

    lax.fori_loop(0, n, step, 0)


def split_coeff(coeff):
    high, low = split(coeff)
    return high, jnp.concatenate([high, low], axis=1)


def project(weights, trail, high, low, c):
    chunks, chunk, columns = trail.shape
    each = chunks // STEPS

    def some(ref):
        return ref[each * c : each * (c + 1)].reshape(each * chunk, ref.shape[2])

    c_high, c_both = weights
    product = dot(some(high), c_both)
    rest = product[:, columns:] + dot(some(low), c_high)
    return (some(trail) - (product[:, :columns] + rest)).reshape(each, chunk, columns)


def whole(c):
    return c % 2 == 0


def factor(work, width):
    def block_step(k, carry):
        first = pl.multiple_of(k * BLOCK, BLOCK)
        rows = work[pl.ds(first, BLOCK), :]
        row_at = lax.broadcasted_iota(jnp.int32, (BLOCK, 1), 0)
        lane_at = lax.broadcasted_iota(jnp.int32, (BLOCK, width), 1)
        for j in range(BLOCK):
            column = jnp.sum(
                jnp.where(lane_at == first + j, rows[:, :width], 0.0), axis=1, keepdims=True
            )
            pivot = column[j : j + 1, :]
            scale = lax.rsqrt(pivot)
            scale = scale * (1.5 - 0.5 * pivot * scale * scale)
            pivot_row = rows[j : j + 1, :] * scale
            below = jnp.where(row_at > j, column * scale, 0.0)
            rows = jnp.where(row_at == j, pivot_row, rows - below * pivot_row)
        work[pl.ds(first, BLOCK), :] = rows
        later = jnp.where(lane_at >= first + BLOCK, rows[:, :width], 0.0)
        work[...] -= exact(later, rows, ((0,), (0,)))
        return carry

    lax.fori_loop(0, width // BLOCK, block_step, 0)


def kernel(
    groups, ring, chunk, late,
    panel, trailing, r_factor, r_cross, coeff, trail, high, low,
    held, turned, gram, gram_in, gram_y, gram_all, work, both, both_high, both_low,
    acc, cross_out, cross_in, cross_all, guest, guest_out, guest_in, guest_sum, guest_part,
    own_sem, trail_sem,
    send_r, send_l, recv_l, recv_r, pass_send_r, pass_send_l, pass_recv_l, pass_recv_r,
    small_send, small_recv, guest_send, guest_recv, part_send, part_recv, news,
):
    width = panel.shape[1]
    columns = trailing.shape[1]
    own = panel.shape[0] // chunk
    half = own // 2
    early = max(own * 3 // 8, 1)
    chunks = trailing.shape[0] // chunk
    part = width // groups
    edge, cut = half - late - 1, chunk // 2
    late_rows = late * chunk + cut
    me = lax.axis_index("rows")
    y = lax.axis_index("cols")
    sides = trailing.shape[0] // panel.shape[0]
    right = lax.rem(y + 1, sides)
    left = lax.rem(y + sides - 1, sides)
    across = lax.rem(y + 2, sides)

    def load_panel(c):
        return pltpu.make_async_copy(
            panel.at[pl.ds(c * chunk, chunk)], held.at[y * own + c], own_sem.at[c]
        )

    def load_trail(c):
        return pltpu.make_async_copy(
            trailing.at[pl.ds(c * chunk, chunk)], trail.at[c], trail_sem.at[c]
        )

    core, z, x = lax.rem(me, 2), lax.rem(me // 2, ring), me // (2 * ring)

    def at_xz(dx, dz, other):
        return (lax.rem(x + dx, ring) * ring + lax.rem(z + dz, ring)) * 2 + lax.rem(core + other, 2)

    def peer(i):
        return at_xz(ring // 2 + i // (2 * ring), ring // 2 + lax.rem(i // 2, ring), lax.rem(i, 2))

    itself = (ring - ring // 2) * (2 * ring + 2)

    def each_peer(body):
        loop(itself, lambda i: body(peer(i)))
        loop(groups - 1 - itself, lambda i: body(peer(itself + 1 + i)))

    def side(d):
        return lax.rem(y + d + 1, sides)

    def tell(sem, **to):
        pl.semaphore_signal(sem, inc=1, device_id=to, device_id_type=MESH)

    def tell_x(sem):
        tell(sem, rows=at_xz(1, 0, 0))
        tell(sem, rows=at_xz(ring - 1, 0, 0))

    def tell_y(sem):
        tell(sem, cols=right)
        tell(sem, cols=left)

    def tell_z(sem):
        tell(sem, rows=at_xz(0, 1, 0))
        tell(sem, rows=at_xz(0, ring - 1, 0))

    barrier = pltpu.get_barrier_semaphore()
    tell_y(barrier)
    tell_x(barrier)
    tell_z(barrier)
    tell(barrier, rows=at_xz(0, 0, 1))
    loop(own, lambda c: load_panel(c).start())
    pl.semaphore_wait(barrier, 7)
    tell_x(news.at[0])
    tell_y(news.at[1])

    def copy_y(src, dst, send, recv, to):
        return pltpu.make_async_remote_copy(
            src_ref=src, dst_ref=dst, send_sem=send, recv_sem=recv,
            device_id={"cols": to}, device_id_type=MESH)

    def to_right(c):
        return copy_y(panel.at[pl.ds(c * chunk, chunk)], held.at[y * own + c],
                      send_r.at[c], recv_l.at[c], right)

    def to_left(c):
        return copy_y(panel.at[pl.ds(c * chunk, chunk)], held.at[y * own + c],
                      send_l.at[c], recv_r.at[c], left)

    def from_left(c):
        return copy_y(held.at[left * own + c], held.at[left * own + c],
                      send_r.at[c], recv_l.at[c], right)

    def from_right(c):
        return copy_y(held.at[right * own + c], held.at[right * own + c],
                      send_l.at[c], recv_r.at[c], left)

    def piece(at, c, rows):
        return held.at[at + c] if rows is None else held.at[at + c, pl.ds(rows * cut, cut)]

    def pass_right(c, rows=None):
        ref, sem = piece(left * own, c, rows), half if rows == 1 else c
        return copy_y(ref, ref, pass_send_r.at[sem], pass_recv_l.at[sem], right)

    def pass_left(c, rows=None):
        ref, sem = piece(right * own + half, c, rows), half if rows == 1 else c
        return copy_y(ref, ref, pass_send_l.at[sem], pass_recv_r.at[sem], left)

    def passed_left(c, rows=None):
        ref, sem = piece(across * own, c, rows), half if rows == 1 else c
        return copy_y(ref, ref, pass_send_r.at[sem], pass_recv_l.at[sem], right)

    def passed_right(c, rows=None):
        ref, sem = piece(across * own + half, c, rows), half if rows == 1 else c
        return copy_y(ref, ref, pass_send_l.at[sem], pass_recv_r.at[sem], left)

    def guest_left():
        rows = trailing.at[pl.ds((across * own + half) * chunk - late_rows, late_rows)]
        return copy_y(rows, guest.at[0], guest_send.at[0], guest_recv.at[0], left)

    def guest_right():
        rows = trailing.at[pl.ds((across * own + own) * chunk - late_rows, late_rows)]
        return copy_y(rows, guest.at[1], guest_send.at[1], guest_recv.at[1], right)

    def part_right():
        return copy_y(guest_sum.at[0], guest_part.at[0], part_send.at[0], part_recv.at[0], right)

    def part_left():
        return copy_y(guest_sum.at[1], guest_part.at[1], part_send.at[1], part_recv.at[1], left)

    def send_own(c):
        to_right(c).start()
        to_left(lax.rem(c + half, own)).start()

    loop(early, send_own)
    loop(chunks, lambda c: load_trail(c).start())

    gram[...] = jnp.zeros_like(gram)

    def gram_step(c):
        load_panel(c).wait()
        at = y * own + c
        x = held[at]
        x_high, x_low = split(x)
        high[at] = x_high
        low[at] = x_low
        gram[...] += exact(x, x, ((0,), (0,)))

    loop(own, gram_step)
    pl.semaphore_wait(news.at[0], 2)
    tell_z(news.at[2])

    def spread(src_of, dst, stage):
        def one(to):
            pltpu.make_async_remote_copy(
                src_ref=src_of(to), dst_ref=dst.at[me],
                send_sem=small_send.at[stage], recv_sem=small_recv.at[stage],
                device_id={"rows": to}, device_id_type=MESH).start()

        each_peer(one)

    def spread_wait(dst, stage):
        some = dst.at[pl.ds(0, groups - 1)]
        everything = pltpu.make_async_remote_copy(
            src_ref=some, dst_ref=some,
            send_sem=small_send.at[stage], recv_sem=small_recv.at[stage],
            device_id={"rows": at_xz(1, 0, 0)}, device_id_type=MESH)
        everything.wait()

    def turn(c):
        load_trail(c).wait()
        t_high, t_low = split(trail[c].T)
        turned[c, :columns, :] = t_high
        turned[c, columns:, :] = t_low

    third = chunks // 3
    loop(third, turn)
    pl.semaphore_wait(news.at[2], 2)
    tell_z(news.at[3])
    loop(third, lambda c: turn(third + c))
    pl.semaphore_wait(news.at[3], 2)
    tell(news.at[4], rows=at_xz(0, 0, 1))
    loop(chunks - 2 * third, lambda c: turn(2 * third + c))
    pl.semaphore_wait(news.at[4], 1)
    pl.semaphore_wait(news.at[1], 2)

    spread(lambda to: gram.at[pl.ds(pl.multiple_of(to * part, 8), part)], gram_in, 0)
    gram_in[me] = gram[pl.ds(pl.multiple_of(me * part, 8), part), :]

    spread_wait(gram_in, 0)
    gram_y[y] = jnp.sum(gram_in[...], axis=0)

    def over_y(d):
        return copy_y(gram_y.at[y], gram_y.at[y], small_send.at[1], small_recv.at[1], side(d))

    loop(sides - 1, lambda d: over_y(d).start())
    guest_left().start()
    guest_right().start()
    loop(own - early, lambda c: send_own(early + c))

    acc[...] = jnp.zeros_like(acc)

    def cross_of(t_both, x_high, x_low):
        product = dot(t_both, x_high)
        return product[:columns] + (product[columns:] + dot(t_both[:columns], x_low))

    def add_cross(at):
        acc[...] += cross_of(turned[at], high[at], low[at])

    def lay(out, first, sums):
        for side_at in range(width // 128):
            out[pl.ds(side_at * columns, columns), first : first + columns] = (
                sums[:, side_at * 128 : side_at * 128 + 128])

    def mine(ref):
        return ref[pl.ds(pl.multiple_of(me * part, 8), part), :]

    def slice_for(ref):
        return lambda to: ref.at[pl.ds(pl.multiple_of(to * part, 8), part)]

    loop(own, lambda c: add_cross(y * own + c))

    some = gram_y.at[pl.ds(0, sides - 1)]
    copy_y(some, some, small_send.at[1], small_recv.at[1], right).wait()
    gram_all[me] = jnp.sum(gram_y[...], axis=0)
    spread(lambda to: gram_all.at[me], gram_all, 2)
    spread_wait(gram_all, 2)

    row_at = lax.broadcasted_iota(jnp.int32, (width, width), 0)
    col_at = lax.broadcasted_iota(jnp.int32, (width, width), 1)
    work[:, :width] = gram_all[...].reshape(width, width)
    work[:, width:] = jnp.where(row_at == col_at, 1.0, 0.0)
    factor(work, width)
    r_factor[...] = jnp.where(row_at <= col_at, work[:, :width], 0.0)
    inverse = work[:, width:]
    both[:width, :] = inverse
    both[width:, :] = exact(inverse, inverse, ((0,), (0,)))
    both_high[...], both_low[...] = split(both[...])

    def take(at):
        x_high, x_low = split(held[at])
        high[at] = x_high
        low[at] = x_low
        add_cross(at)

    def first_half(c, rows=None):
        from_left(c).wait_recv()
        pass_right(c, rows).start()
        from_right(half + c).wait_recv()
        pass_left(c, rows).start()
        take(left * own + c)
        take(right * own + half + c)

    def guests():
        for c in range(half - late, half):
            from_left(c).wait_recv()
            take(left * own + c)
            from_right(half + c).wait_recv()
            take(right * own + half + c)
        for place, at in ((0, left * own + half), (1, right * own + own)):
            copy_y(guest.at[place], guest.at[place],
                   guest_send.at[place], guest_recv.at[place], right).wait_recv()
            t_both = jnp.concatenate(split(guest[place].T), axis=0)
            x_high, x_low = (
                jnp.concatenate([
                    ref[at - late - 1, chunk - cut :],
                    ref[pl.ds(at - late, late)].reshape(late * chunk, width),
                ], axis=0)
                for ref in (high, low))
            lay(guest_out, place * columns, cross_of(t_both, x_high, x_low))
        spread(slice_for(guest_out), guest_in, 5)
        guest_in[me] = mine(guest_out)

    def second_half(c):
        from_left(half + c).wait_recv()
        take(left * own + half + c)
        from_right(c).wait_recv()
        take(right * own + c)

    def keep_cut(at, rows):
        x_high, x_low = split(held[at, rows])
        high[at, rows] = x_high
        low[at, rows] = x_low
        return x_high, x_low

    def take_cut(at):
        x_high, x_low = keep_cut(at, slice(0, cut))
        acc[...] += cross_of(turned[at, :, :cut], x_high, x_low)

    def passed(c):
        passed_left(c).wait_recv()
        take(across * own + c)
        passed_right(c).wait_recv()
        take(across * own + half + c)

    loop(edge, first_half)
    first_half(edge, 0)
    guests()
    loop(half, second_half)
    spread_wait(guest_in, 5)
    sums = jnp.sum(guest_in[...], axis=0)
    guest_sum[0] = sums[:, :columns]
    guest_sum[1] = sums[:, columns:]
    part_right().start()
    part_left().start()
    pass_right(edge, 1).start()
    pass_left(edge, 1).start()
    for c in range(edge + 1, half):
        pass_right(c).start()
        pass_left(c).start()

    def finish(c):
        to_right(c).wait_send()
        to_left(c).wait_send()

    loop(own, finish)
    for copy in (guest_left(), guest_right()):
        copy.wait_send()
    loop(edge, passed)
    passed_left(edge, 0).wait_recv()
    take_cut(across * own + edge)
    passed_right(edge, 0).wait_recv()
    take_cut(across * own + half + edge)

    lay(cross_out, 0, acc[...])
    spread(slice_for(cross_out), cross_in, 3)
    cross_in[me] = mine(cross_out)
    for place in range(2):
        copy_y(guest_part.at[place], guest_part.at[place],
               part_send.at[place], part_recv.at[place], right).wait_recv()
    spread_wait(cross_in, 3)
    cross_all[me] = jnp.sum(cross_in[...], axis=0) + (guest_part[0] + guest_part[1])
    spread(lambda to: cross_all.at[me], cross_all, 4)

    def finish_passed(c, rows=None):
        pass_right(c, rows).wait_send()
        pass_left(c, rows).wait_send()

    loop(edge, finish_passed)
    finish_passed(edge, 0)
    for copy in (part_right(), part_left()):
        copy.wait_send()
    spread_wait(cross_all, 4)

    flat = cross_all[...].reshape(width, columns)
    cross = jnp.concatenate([flat[:columns], flat[columns:]], axis=1)
    x_high, x_low = split(cross)
    x_both = jnp.concatenate([x_high, x_low], axis=0)

    def solve(rows):
        product = dot_turned(both_high[rows, :], x_both)
        rest = product[:, columns:] + dot_turned(both_low[rows, :], x_high)
        return product[:, :columns] + rest

    solved = solve(slice(width, 2 * width))
    coeff[...] = solved
    weights = split_coeff(solved)
    each = chunks // STEPS
    for c in range(STEPS):
        if whole(c):
            trail[each * c : each * (c + 1)] = project(weights, trail, high, low, c)
    r_cross[...] = solve(slice(0, width))

    def keep(at):
        high[at], low[at] = split(held[at])

    passed_left(edge, 1).wait_recv()
    keep_cut(across * own + edge, slice(cut, chunk))
    passed_right(edge, 1).wait_recv()
    keep_cut(across * own + half + edge, slice(cut, chunk))
    for c in range(edge + 1, half):
        passed_left(c).wait_recv()
        keep(across * own + c)
        passed_right(c).wait_recv()
        keep(across * own + half + c)

    finish_passed(edge, 1)
    loop(late, lambda c: finish_passed(edge + 1 + c))


def residual_kernel(
    r_factor_in, r_cross_in, coeff, trail, high, low, r_factor, r_cross, residual, staged, out_sem, small_sem
):
    each = trail.shape[0] // STEPS

    def store(c, rows):
        return pltpu.make_async_copy(
            rows, residual.at[pl.ds(each * c, each)], out_sem.at[c]
        )

    def rows_of(c):
        return trail.at[pl.ds(each * c, each)] if whole(c) else staged.at[c // 2]

    small = (
        pltpu.make_async_copy(r_factor_in, r_factor, small_sem.at[0]),
        pltpu.make_async_copy(r_cross_in, r_cross, small_sem.at[1]),
    )
    for c in range(STEPS):
        if whole(c):
            store(c, rows_of(c)).start()
    for copy in small:
        copy.start()
    weights = split_coeff(coeff[...])
    for c in range(STEPS):
        if not whole(c):
            staged[c // 2] = project(weights, trail, high, low, c)
            store(c, rows_of(c)).start()
    for c in range(STEPS):
        store(c, rows_of(c)).wait()
    for copy in small:
        copy.wait()


def per_device(groups, chunk, late, panel, trailing):
    ring = math.isqrt(groups // 2)
    rows, width = panel.shape
    total, columns = trailing.shape
    own, chunks, part = rows // chunk, total // chunk, width // groups
    half = own // 2
    sides = total // rows
    f32, bf16 = jnp.float32, jnp.bfloat16
    dma = pltpu.SemaphoreType.DMA
    hbm = pl.BlockSpec(memory_space=pl.ANY)
    vmem = pl.BlockSpec(memory_space=pltpu.VMEM)
    r_factor, r_cross, coeff, trail, high, low = pl.pallas_call(
        functools.partial(kernel, groups, ring, chunk, late),
        out_shape=(
            pltpu.VMEM((width, width), f32),
            pltpu.VMEM((width, columns), f32),
            pltpu.VMEM((width, columns), f32),
            pltpu.VMEM((chunks, chunk, columns), f32),
            pltpu.VMEM((chunks, chunk, width), bf16),
            pltpu.VMEM((chunks, chunk, width), bf16),
        ),
        in_specs=[hbm] * 2,
        out_specs=(vmem,) * 6,
        scratch_shapes=[
            pltpu.VMEM((chunks, chunk, width), f32),
            pltpu.VMEM((chunks, 2 * columns, chunk), bf16),
            pltpu.VMEM((width, width), f32),
            pltpu.VMEM((groups, part, width), f32),
            pltpu.VMEM((sides, part, width), f32),
            pltpu.VMEM((groups, part, width), f32),
            pltpu.VMEM((width, 2 * width), f32),
            pltpu.VMEM((2 * width, width), f32),
            pltpu.VMEM((2 * width, width), bf16),
            pltpu.VMEM((2 * width, width), bf16),
            pltpu.VMEM((columns, width), f32),
            pltpu.VMEM((width, columns), f32),
            pltpu.VMEM((groups, part, columns), f32),
            pltpu.VMEM((groups, part, columns), f32),
            pltpu.VMEM((2, late * chunk + chunk // 2, columns), f32),
            pltpu.VMEM((width, 2 * columns), f32),
            pltpu.VMEM((groups, part, 2 * columns), f32),
            pltpu.VMEM((2, part, columns), f32),
            pltpu.VMEM((2, part, columns), f32),
            dma((own,)), dma((chunks,)),
            dma((own,)), dma((own,)), dma((own,)), dma((own,)),
            dma((half + 1,)), dma((half + 1,)), dma((half + 1,)), dma((half + 1,)),
            dma((6,)), dma((6,)), dma((2,)), dma((2,)), dma((2,)), dma((2,)), pltpu.SemaphoreType.REGULAR((5,)),
        ],
        compiler_params=pltpu.CompilerParams(
            collective_id=0, has_side_effects=True, vmem_limit_bytes=34 * 2**20
        ),
    )(panel, trailing)
    r_factor, r_cross, residual = pl.pallas_call(
        residual_kernel,
        out_shape=(
            jax.ShapeDtypeStruct((width, width), f32),
            jax.ShapeDtypeStruct((width, columns), f32),
            jax.ShapeDtypeStruct((chunks, chunk, columns), f32),
        ),
        in_specs=[vmem] * 6,
        out_specs=(hbm,) * 3,
        scratch_shapes=[pltpu.VMEM((STEPS // 2, chunks // STEPS, chunk, columns), f32), dma((STEPS,)), dma((2,))],
        compiler_params=pltpu.CompilerParams(vmem_limit_bytes=10 * 2**20),
    )(r_factor, r_cross, coeff, trail, high, low)
    return r_factor, r_cross, residual.reshape(total, columns)


def solution(mesh):
    return jax.shard_map(
        functools.partial(per_device, mesh.shape["rows"], CHUNK, LATE),
        mesh=mesh,
        in_specs=(P(("rows", "cols"), None), P("rows", "cols")),
        out_specs=(P(), P(None, "cols"), P("rows", "cols")),
        check_vma=False,
    )
```

```python
import functools
import math

import jax
import jax.numpy as jnp
from jax import lax
from jax.experimental import pallas as pl
from jax.experimental.pallas import tpu as pltpu
from jax.sharding import PartitionSpec as P

MESH = pl.DeviceIdType.MESH
CHUNK = 512
LATE = 1
CUT = 2
STEPS = 16
BLOCK = 32


def split(x):
    high = x.astype(jnp.bfloat16)
    return high, (x - high.astype(jnp.float32)).astype(jnp.bfloat16)


def dot(a, b):
    return jnp.dot(a, b, preferred_element_type=jnp.float32)


def dot_turned(a, b):
    return lax.dot_general(a, b, (((1,), (1,)), ((), ())), preferred_element_type=jnp.float32)


def exact(a, b, dims):
    return lax.dot_general(
        a, b, (dims, ((), ())), precision=lax.Precision.HIGHEST, preferred_element_type=jnp.float32
    )


def loop(n, body):
    def step(i, carry):
        body(i)
        return carry

    lax.fori_loop(0, n, step, 0)


def split_coeff(coeff):
    high, low = split(coeff)
    return high, jnp.concatenate([high, low], axis=1)


def project(weights, trail, high, low, c):
    chunks, chunk, columns = trail.shape
    each = chunks // STEPS

    def some(ref):
        return ref[each * c : each * (c + 1)].reshape(each * chunk, ref.shape[2])

    c_high, c_both = weights
    product = dot(some(high), c_both)
    rest = product[:, columns:] + dot(some(low), c_high)
    return (some(trail) - (product[:, :columns] + rest)).reshape(each, chunk, columns)


def whole(c):
    return c % 2 == 0


def factor(work, width):
    def block_step(k, carry):
        first = pl.multiple_of(k * BLOCK, BLOCK)
        rows = work[pl.ds(first, BLOCK), :]
        row_at = lax.broadcasted_iota(jnp.int32, (BLOCK, 1), 0)
        lane_at = lax.broadcasted_iota(jnp.int32, (BLOCK, width), 1)
        for j in range(BLOCK):
            column = jnp.sum(
                jnp.where(lane_at == first + j, rows[:, :width], 0.0), axis=1, keepdims=True
            )
            pivot = column[j : j + 1, :]
            scale = lax.rsqrt(pivot)
            scale = scale * (1.5 - 0.5 * pivot * scale * scale)
            pivot_row = rows[j : j + 1, :] * scale
            below = jnp.where(row_at > j, column * scale, 0.0)
            rows = jnp.where(row_at == j, pivot_row, rows - below * pivot_row)
        work[pl.ds(first, BLOCK), :] = rows
        later = jnp.where(lane_at >= first + BLOCK, rows[:, :width], 0.0)
        work[...] -= exact(later, rows, ((0,), (0,)))
        return carry

    lax.fori_loop(0, width // BLOCK, block_step, 0)


def kernel(
    groups, ring, chunk, late,
    panel, trailing, r_factor, r_cross, coeff, trail, high, low,
    held, turned, gram, gram_in, gram_y, gram_all, work, both, both_high, both_low,
    acc, cross_out, cross_in, cross_all, guest, guest_out, guest_in, guest_sum, guest_part,
    own_sem, trail_sem,
    send_r, send_l, recv_l, recv_r, pass_send_r, pass_send_l, pass_recv_l, pass_recv_r,
    small_send, small_recv, guest_send, guest_recv, part_send, part_recv, news,
):
    width = panel.shape[1]
    columns = trailing.shape[1]
    own = panel.shape[0] // chunk
    half = own // 2
    early = max(own * 3 // 8, 1)
    chunks = trailing.shape[0] // chunk
    part = width // groups
    edge, cut = half - late - 1, chunk // CUT
    late_rows = late * chunk + cut
    me = lax.axis_index("rows")
    y = lax.axis_index("cols")
    sides = trailing.shape[0] // panel.shape[0]
    right = lax.rem(y + 1, sides)
    left = lax.rem(y + sides - 1, sides)
    across = lax.rem(y + 2, sides)

    def load_panel(c):
        return pltpu.make_async_copy(
            panel.at[pl.ds(c * chunk, chunk)], held.at[y * own + c], own_sem.at[c]
        )

    def load_trail(c):
        return pltpu.make_async_copy(
            trailing.at[pl.ds(c * chunk, chunk)], trail.at[c], trail_sem.at[c]
        )

    core, z, x = lax.rem(me, 2), lax.rem(me // 2, ring), me // (2 * ring)

    def at_xz(dx, dz, other):
        return (lax.rem(x + dx, ring) * ring + lax.rem(z + dz, ring)) * 2 + lax.rem(core + other, 2)

    def peer(i):
        return at_xz(ring // 2 + i // (2 * ring), ring // 2 + lax.rem(i // 2, ring), lax.rem(i, 2))

    itself = (ring - ring // 2) * (2 * ring + 2)

    far = sorted(
        ((dx, dz, other) for dx in range(ring) for dz in range(ring) for other in range(2)),
        key=lambda at: -min(at[0], ring - at[0]) - min(at[1], ring - at[1]))

    def each_far(body):
        for at in far:
            if any(at):
                body(at_xz(*at))

    def each_peer(body):
        loop(itself, lambda i: body(peer(i)))
        loop(groups - 1 - itself, lambda i: body(peer(itself + 1 + i)))

    def side(d):
        return lax.rem(y + d + 1, sides)

    def tell(sem, **to):
        pl.semaphore_signal(sem, inc=1, device_id=to, device_id_type=MESH)

    def tell_x(sem):
        tell(sem, rows=at_xz(1, 0, 0))
        tell(sem, rows=at_xz(ring - 1, 0, 0))

    def tell_y(sem):
        tell(sem, cols=right)
        tell(sem, cols=left)

    def tell_z(sem):
        tell(sem, rows=at_xz(0, 1, 0))
        tell(sem, rows=at_xz(0, ring - 1, 0))

    barrier = pltpu.get_barrier_semaphore()
    tell_y(barrier)
    tell_x(barrier)
    tell_z(barrier)
    tell(barrier, rows=at_xz(0, 0, 1))
    loop(own, lambda c: load_panel(c).start())
    pl.semaphore_wait(barrier, 7)
    tell_x(news.at[0])
    tell_y(news.at[1])

    def copy_y(src, dst, send, recv, to):
        return pltpu.make_async_remote_copy(
            src_ref=src, dst_ref=dst, send_sem=send, recv_sem=recv,
            device_id={"cols": to}, device_id_type=MESH)

    def to_right(c):
        return copy_y(panel.at[pl.ds(c * chunk, chunk)], held.at[y * own + c],
                      send_r.at[c], recv_l.at[c], right)

    def to_left(c):
        return copy_y(panel.at[pl.ds(c * chunk, chunk)], held.at[y * own + c],
                      send_l.at[c], recv_r.at[c], left)

    def from_left(c):
        return copy_y(held.at[left * own + c], held.at[left * own + c],
                      send_r.at[c], recv_l.at[c], right)

    def from_right(c):
        return copy_y(held.at[right * own + c], held.at[right * own + c],
                      send_l.at[c], recv_r.at[c], left)

    def piece(at, c, rows):
        if rows is None:
            return held.at[at + c]
        return held.at[at + c, pl.ds(0, chunk - cut) if rows == 0 else pl.ds(chunk - cut, cut)]

    def pass_right(c, rows=None):
        ref, sem = piece(left * own, c, rows), half if rows == 1 else c
        return copy_y(ref, ref, pass_send_r.at[sem], pass_recv_l.at[sem], right)

    def pass_left(c, rows=None):
        ref, sem = piece(right * own + half, c, rows), half if rows == 1 else c
        return copy_y(ref, ref, pass_send_l.at[sem], pass_recv_r.at[sem], left)

    def passed_left(c, rows=None):
        ref, sem = piece(across * own, c, rows), half if rows == 1 else c
        return copy_y(ref, ref, pass_send_r.at[sem], pass_recv_l.at[sem], right)

    def passed_right(c, rows=None):
        ref, sem = piece(across * own + half, c, rows), half if rows == 1 else c
        return copy_y(ref, ref, pass_send_l.at[sem], pass_recv_r.at[sem], left)

    def guest_left():
        rows = trailing.at[pl.ds((across * own + half) * chunk - late_rows, late_rows)]
        return copy_y(rows, guest.at[0], guest_send.at[0], guest_recv.at[0], left)

    def guest_right():
        rows = trailing.at[pl.ds((across * own + own) * chunk - late_rows, late_rows)]
        return copy_y(rows, guest.at[1], guest_send.at[1], guest_recv.at[1], right)

    def part_right():
        return copy_y(guest_sum.at[0], guest_part.at[0], part_send.at[0], part_recv.at[0], right)

    def part_left():
        return copy_y(guest_sum.at[1], guest_part.at[1], part_send.at[1], part_recv.at[1], left)

    def send_own(c):
        to_right(c).start()
        to_left(lax.rem(c + half, own)).start()

    loop(early, send_own)
    loop(chunks, lambda c: load_trail(c).start())

    gram[...] = jnp.zeros_like(gram)

    def gram_step(c):
        load_panel(c).wait()
        at = y * own + c
        x = held[at]
        x_high, x_low = split(x)
        high[at] = x_high
        low[at] = x_low
        gram[...] += exact(x, x, ((0,), (0,)))

    loop(own, gram_step)
    pl.semaphore_wait(news.at[0], 2)
    tell_z(news.at[2])

    def spread(src_of, dst, stage, each=None):
        def one(to):
            pltpu.make_async_remote_copy(
                src_ref=src_of(to), dst_ref=dst.at[me],
                send_sem=small_send.at[stage], recv_sem=small_recv.at[stage],
                device_id={"rows": to}, device_id_type=MESH).start()

        (each or each_peer)(one)

    def spread_wait(dst, stage):
        some = dst.at[pl.ds(0, groups - 1)]
        everything = pltpu.make_async_remote_copy(
            src_ref=some, dst_ref=some,
            send_sem=small_send.at[stage], recv_sem=small_recv.at[stage],
            device_id={"rows": at_xz(1, 0, 0)}, device_id_type=MESH)
        everything.wait()

    def turn(c):
        load_trail(c).wait()
        t_high, t_low = split(trail[c].T)
        turned[c, :columns, :] = t_high
        turned[c, columns:, :] = t_low

    third = chunks // 3
    loop(third, turn)
    pl.semaphore_wait(news.at[2], 2)
    tell_z(news.at[3])
    loop(third, lambda c: turn(third + c))
    pl.semaphore_wait(news.at[3], 2)
    tell(news.at[4], rows=at_xz(0, 0, 1))
    loop(chunks - 2 * third, lambda c: turn(2 * third + c))
    pl.semaphore_wait(news.at[4], 1)
    pl.semaphore_wait(news.at[1], 2)

    spread(lambda to: gram.at[pl.ds(pl.multiple_of(to * part, 8), part)], gram_in, 0)
    gram_in[me] = gram[pl.ds(pl.multiple_of(me * part, 8), part), :]

    spread_wait(gram_in, 0)
    gram_y[y] = jnp.sum(gram_in[...], axis=0)

    def over_y(d):
        return copy_y(gram_y.at[y], gram_y.at[y], small_send.at[1], small_recv.at[1], side(d))

    loop(sides - 1, lambda d: over_y(d).start())
    guest_left().start()
    guest_right().start()
    loop(own - early, lambda c: send_own(early + c))

    acc[...] = jnp.zeros_like(acc)

    def cross_of(t_both, x_high, x_low):
        product = dot(t_both, x_high)
        return product[:columns] + (product[columns:] + dot(t_both[:columns], x_low))

    def add_cross(at):
        acc[...] += cross_of(turned[at], high[at], low[at])

    def lay(out, first, sums):
        for side_at in range(width // 128):
            out[pl.ds(side_at * columns, columns), first : first + columns] = (
                sums[:, side_at * 128 : side_at * 128 + 128])

    def mine(ref):
        return ref[pl.ds(pl.multiple_of(me * part, 8), part), :]

    def slice_for(ref):
        return lambda to: ref.at[pl.ds(pl.multiple_of(to * part, 8), part)]

    loop(own, lambda c: add_cross(y * own + c))

    some = gram_y.at[pl.ds(0, sides - 1)]
    copy_y(some, some, small_send.at[1], small_recv.at[1], right).wait()
    gram_all[me] = jnp.sum(gram_y[...], axis=0)
    spread(lambda to: gram_all.at[me], gram_all, 2)
    spread_wait(gram_all, 2)

    row_at = lax.broadcasted_iota(jnp.int32, (width, width), 0)
    col_at = lax.broadcasted_iota(jnp.int32, (width, width), 1)
    work[:, :width] = gram_all[...].reshape(width, width)
    work[:, width:] = jnp.where(row_at == col_at, 1.0, 0.0)
    factor(work, width)
    r_factor[...] = jnp.where(row_at <= col_at, work[:, :width], 0.0)
    inverse = work[:, width:]
    both[:width, :] = inverse
    both[width:, :] = exact(inverse, inverse, ((0,), (0,)))
    both_high[...], both_low[...] = split(both[...])

    def take(at):
        x_high, x_low = split(held[at])
        high[at] = x_high
        low[at] = x_low
        add_cross(at)

    def first_half(c, rows=None):
        from_left(c).wait_recv()
        pass_right(c, rows).start()
        from_right(half + c).wait_recv()
        pass_left(c, rows).start()
        take(left * own + c)
        take(right * own + half + c)

    def guests():
        for c in range(half - late, half):
            from_left(c).wait_recv()
            take(left * own + c)
            from_right(half + c).wait_recv()
            take(right * own + half + c)
        for place, at in ((0, left * own + half), (1, right * own + own)):
            copy_y(guest.at[place], guest.at[place],
                   guest_send.at[place], guest_recv.at[place], right).wait_recv()
            t_both = jnp.concatenate(split(guest[place].T), axis=0)
            x_high, x_low = (
                jnp.concatenate([
                    ref[at - late - 1, chunk - cut :],
                    ref[pl.ds(at - late, late)].reshape(late * chunk, width),
                ], axis=0)
                for ref in (high, low))
            lay(guest_out, place * columns, cross_of(t_both, x_high, x_low))
        spread(slice_for(guest_out), guest_in, 5)
        guest_in[me] = mine(guest_out)

    def second_half(c):
        from_left(half + c).wait_recv()
        take(left * own + half + c)
        from_right(c).wait_recv()
        take(right * own + c)

    def keep_cut(at, rows):
        x_high, x_low = split(held[at, rows])
        high[at, rows] = x_high
        low[at, rows] = x_low
        return x_high, x_low

    def take_cut(at):
        x_high, x_low = keep_cut(at, slice(0, chunk - cut))
        acc[...] += cross_of(turned[at, :, : chunk - cut], x_high, x_low)

    def passed(c):
        passed_left(c).wait_recv()
        take(across * own + c)
        passed_right(c).wait_recv()
        take(across * own + half + c)

    loop(edge, first_half)
    first_half(edge, 0)
    guests()
    loop(half, second_half)
    spread_wait(guest_in, 5)
    sums = jnp.sum(guest_in[...], axis=0)
    guest_sum[0] = sums[:, :columns]
    guest_sum[1] = sums[:, columns:]
    part_right().start()
    part_left().start()
    for c in range(edge + 1, half):
        pass_right(c).start()
        pass_left(c).start()
    pass_right(edge, 1).start()
    pass_left(edge, 1).start()

    def finish(c):
        to_right(c).wait_send()
        to_left(c).wait_send()

    loop(own, finish)
    for copy in (guest_left(), guest_right()):
        copy.wait_send()
    loop(edge, passed)
    passed_left(edge, 0).wait_recv()
    take_cut(across * own + edge)
    passed_right(edge, 0).wait_recv()
    take_cut(across * own + half + edge)

    lay(cross_out, 0, acc[...])
    spread(slice_for(cross_out), cross_in, 3, each_far)
    cross_in[me] = mine(cross_out)
    for place in range(2):
        copy_y(guest_part.at[place], guest_part.at[place],
               part_send.at[place], part_recv.at[place], right).wait_recv()
    spread_wait(cross_in, 3)
    cross_all[me] = jnp.sum(cross_in[...], axis=0) + (guest_part[0] + guest_part[1])
    spread(lambda to: cross_all.at[me], cross_all, 4, each_far)

    def finish_passed(c, rows=None):
        pass_right(c, rows).wait_send()
        pass_left(c, rows).wait_send()

    loop(edge, finish_passed)
    finish_passed(edge, 0)
    for copy in (part_right(), part_left()):
        copy.wait_send()
    spread_wait(cross_all, 4)

    flat = cross_all[...].reshape(width, columns)
    cross = jnp.concatenate([flat[:columns], flat[columns:]], axis=1)
    x_high, x_low = split(cross)
    x_both = jnp.concatenate([x_high, x_low], axis=0)

    def solve(rows):
        product = dot_turned(both_high[rows, :], x_both)
        rest = product[:, columns:] + dot_turned(both_low[rows, :], x_high)
        return product[:, :columns] + rest

    solved = solve(slice(width, 2 * width))
    coeff[...] = solved
    weights = split_coeff(solved)
    each = chunks // STEPS
    for c in range(STEPS):
        if whole(c):
            trail[each * c : each * (c + 1)] = project(weights, trail, high, low, c)
    r_cross[...] = solve(slice(0, width))

    def keep(at):
        high[at], low[at] = split(held[at])

    for c in range(edge + 1, half):
        passed_left(c).wait_recv()
        keep(across * own + c)
        passed_right(c).wait_recv()
        keep(across * own + half + c)
    passed_left(edge, 1).wait_recv()
    keep_cut(across * own + edge, slice(chunk - cut, chunk))
    passed_right(edge, 1).wait_recv()
    keep_cut(across * own + half + edge, slice(chunk - cut, chunk))

    finish_passed(edge, 1)
    loop(late, lambda c: finish_passed(edge + 1 + c))


def residual_kernel(
    r_factor_in, r_cross_in, coeff, trail, high, low, r_factor, r_cross, residual, staged, out_sem, small_sem
):
    each = trail.shape[0] // STEPS

    def store(c, rows):
        return pltpu.make_async_copy(
            rows, residual.at[pl.ds(each * c, each)], out_sem.at[c]
        )

    def rows_of(c):
        return trail.at[pl.ds(each * c, each)] if whole(c) else staged.at[c // 2]

    small = (
        pltpu.make_async_copy(r_factor_in, r_factor, small_sem.at[0]),
        pltpu.make_async_copy(r_cross_in, r_cross, small_sem.at[1]),
    )
    for c in range(STEPS):
        if whole(c):
            store(c, rows_of(c)).start()
    for copy in small:
        copy.start()
    weights = split_coeff(coeff[...])
    for c in range(STEPS):
        if not whole(c):
            staged[c // 2] = project(weights, trail, high, low, c)
            store(c, rows_of(c)).start()
    for c in range(STEPS):
        store(c, rows_of(c)).wait()
    for copy in small:
        copy.wait()


def per_device(groups, chunk, late, panel, trailing):
    ring = math.isqrt(groups // 2)
    rows, width = panel.shape
    total, columns = trailing.shape
    own, chunks, part = rows // chunk, total // chunk, width // groups
    half = own // 2
    sides = total // rows
    f32, bf16 = jnp.float32, jnp.bfloat16
    dma = pltpu.SemaphoreType.DMA
    hbm = pl.BlockSpec(memory_space=pl.ANY)
    vmem = pl.BlockSpec(memory_space=pltpu.VMEM)
    r_factor, r_cross, coeff, trail, high, low = pl.pallas_call(
        functools.partial(kernel, groups, ring, chunk, late),
        out_shape=(
            pltpu.VMEM((width, width), f32),
            pltpu.VMEM((width, columns), f32),
            pltpu.VMEM((width, columns), f32),
            pltpu.VMEM((chunks, chunk, columns), f32),
            pltpu.VMEM((chunks, chunk, width), bf16),
            pltpu.VMEM((chunks, chunk, width), bf16),
        ),
        in_specs=[hbm] * 2,
        out_specs=(vmem,) * 6,
        scratch_shapes=[
            pltpu.VMEM((chunks, chunk, width), f32),
            pltpu.VMEM((chunks, 2 * columns, chunk), bf16),
            pltpu.VMEM((width, width), f32),
            pltpu.VMEM((groups, part, width), f32),
            pltpu.VMEM((sides, part, width), f32),
            pltpu.VMEM((groups, part, width), f32),
            pltpu.VMEM((width, 2 * width), f32),
            pltpu.VMEM((2 * width, width), f32),
            pltpu.VMEM((2 * width, width), bf16),
            pltpu.VMEM((2 * width, width), bf16),
            pltpu.VMEM((columns, width), f32),
            pltpu.VMEM((width, columns), f32),
            pltpu.VMEM((groups, part, columns), f32),
            pltpu.VMEM((groups, part, columns), f32),
            pltpu.VMEM((2, late * chunk + chunk // CUT, columns), f32),
            pltpu.VMEM((width, 2 * columns), f32),
            pltpu.VMEM((groups, part, 2 * columns), f32),
            pltpu.VMEM((2, part, columns), f32),
            pltpu.VMEM((2, part, columns), f32),
            dma((own,)), dma((chunks,)),
            dma((own,)), dma((own,)), dma((own,)), dma((own,)),
            dma((half + 1,)), dma((half + 1,)), dma((half + 1,)), dma((half + 1,)),
            dma((6,)), dma((6,)), dma((2,)), dma((2,)), dma((2,)), dma((2,)), pltpu.SemaphoreType.REGULAR((5,)),
        ],
        compiler_params=pltpu.CompilerParams(
            collective_id=0, has_side_effects=True, vmem_limit_bytes=34 * 2**20
        ),
    )(panel, trailing)
    r_factor, r_cross, residual = pl.pallas_call(
        residual_kernel,
        out_shape=(
            jax.ShapeDtypeStruct((width, width), f32),
            jax.ShapeDtypeStruct((width, columns), f32),
            jax.ShapeDtypeStruct((chunks, chunk, columns), f32),
        ),
        in_specs=[vmem] * 6,
        out_specs=(hbm,) * 3,
        scratch_shapes=[pltpu.VMEM((STEPS // 2, chunks // STEPS, chunk, columns), f32), dma((STEPS,)), dma((2,))],
        compiler_params=pltpu.CompilerParams(vmem_limit_bytes=10 * 2**20),
    )(r_factor, r_cross, coeff, trail, high, low)
    return r_factor, r_cross, residual.reshape(total, columns)


def solution(mesh):
    return jax.shard_map(
        functools.partial(per_device, mesh.shape["rows"], CHUNK, LATE),
        mesh=mesh,
        in_specs=(P(("rows", "cols"), None), P("rows", "cols")),
        out_specs=(P(), P(None, "cols"), P("rows", "cols")),
        check_vma=False,
    )
```
